128 devices in a mesh: view: 16 (over x_hi, z, core), head: 8 (over y, x_lo).
Axes of the slice: x: 4 (x_hi: 2, x_lo: 2; x = x_hi * 2 + x_lo), y: 4, z: 4, core: 2. Of those that a mesh axis runs over, the one named last changes fastest.
Arguments:
- x_tokens: bfloat16 [8192, 3072], P('view'), may hold values from -14 to 14
- w_qkv: bfloat16 [3072, 3, 3072], P(None, None, 'head'), may hold values from -0.109375 to 0.109375
- w_out: bfloat16 [3072, 3072], P(None, 'head'), may hold values from -0.109375 to 0.109375
- grad_out: bfloat16 [8192, 3072], P('view'), may hold values from -1.5 to 1.5
Outputs:
- mixed_out: bfloat16 [8192, 3072], P('view')
- d_input: bfloat16 [8192, 3072], P('view')
- d_w_qkv: float32 [3072, 3, 3072], P('view', None, 'head')
- d_w_out: float32 [3072, 3072], P('view', 'head')
The draws below stay inside these ranges and needn't reach their ends.
All inputs are finite; a program needn't handle non-finite values.
Results may differ from the reference program's by a relative error of at most 0.02.
The reference program's roundings to bfloat16 on the way (of `projected`, `rounded`, `attended`, `d_att`, `d_scores`, `d_query` and `d_projected`) count: a program that leaves them out, or rounds other values in their place, can miss the bound.
Values may be sent and summed in bfloat16 or wider, within the bound.
No kernel may reach another device: no remote copies, remote signals or barrier semaphores. Data moves between devices by JAX's collectives and lax.ppermute only.
A program may use at most 192 MiB of HBM per device.

```python
import math
import jax
import jax.numpy as jnp
from jax import lax

D = 3072
HEADS = 24
TOK = 512
REACH = 2
VIEWS = 16
TOKENS = 8192


def draw_x_tokens(key, part):
    key = jax.random.fold_in(key, 11)
    first_key = jax.random.fold_in(key, 0)
    values = jnp.clip(jax.random.normal(first_key, (TOKENS, D), jnp.float32), -4.0, 4.0)
    return values.astype(jnp.bfloat16)


def block_levels(stream_key, dims, pieces, smallest, high):
    def one(dim, blocks):
        draws = jax.random.uniform(jax.random.fold_in(jax.random.fold_in(stream_key, 6), dim), (blocks,), jnp.float32, smallest / len(pieces), high / len(pieces))
        return jnp.repeat(jnp.exp(draws), dims[dim] // blocks).reshape((-1,) + (1,) * (len(dims) - dim - 1))

    factor_of = one(*pieces[0])
    for cut in pieces[1:]:
        factor_of = factor_of * one(*cut)
    return factor_of


def gaussian(key, shape, scale, bound, pieces=(), kind=jnp.bfloat16):
    entries = scale * jax.random.normal(key, shape, jnp.float32)
    if pieces:
        entries = entries * block_levels(key, shape, pieces, -0.22, 0.18)
    return jnp.clip(entries, -bound, bound).astype(kind)


def setup_inputs(seed: int = 0) -> dict:
    splits = jax.random.split(jax.random.key(seed), 5)
    x_tokens = draw_x_tokens(jax.random.fold_in(splits[4], 71), 0)
    w_qkv = gaussian(splits[1], (D, 3, D), D ** -0.5, 0.109375, ((2, 8),))
    w_out = gaussian(splits[2], (D, D), D ** -0.5, 0.109375, ((1, 8),))
    grad_out = gaussian(splits[3], (TOKENS, D), 0.25, 1.5, ((0, 16),))
    return {"x_tokens": x_tokens, "w_qkv": w_qkv, "w_out": w_out, "grad_out": grad_out}


def neighbours(blocks):
    return jnp.concatenate([jnp.roll(blocks, -offset, axis=0) for offset in range(-REACH, REACH + 1)], axis=1)

def reference(x_tokens, w_qkv, w_out, grad_out):
    head_dim = D // HEADS
    score_scale = 1.0 / math.sqrt(head_dim)
    key_span = 2 * REACH + 1
    w_flat = w_qkv.reshape(D, 3 * D)
    projected = jnp.dot(x_tokens, w_flat, preferred_element_type=jnp.float32).astype(jnp.bfloat16)
    projected = projected.reshape(VIEWS, TOK, 3, HEADS, head_dim)
    queries = projected[:, :, 0]
    key_all = neighbours(projected[:, :, 1])
    value_all = neighbours(projected[:, :, 2])

    def weights_of(query_rows, key_rows):
        scores = jnp.einsum('qhe,khe->hqk', query_rows.astype(jnp.float32), key_rows.astype(jnp.float32)) * score_scale
        return jax.nn.softmax(scores, axis=-1)

    def forward_view(view_items):
        query_rows, key_rows, value_rows = view_items
        soft_weights = weights_of(query_rows, key_rows)
        rounded = lax.optimization_barrier(soft_weights.astype(jnp.bfloat16)).astype(jnp.float32)
        return jnp.einsum('hqk,khe->qhe', rounded, value_rows.astype(jnp.float32)).astype(jnp.bfloat16)
    attended = lax.map(forward_view, (queries, key_all, value_all))
    attended_flat = attended.reshape(TOKENS, D)
    mixed_out = jnp.dot(attended_flat, w_out.T, preferred_element_type=jnp.float32).astype(jnp.bfloat16)
    d_att_flat = jnp.dot(grad_out, w_out, preferred_element_type=jnp.float32).astype(jnp.bfloat16)
    d_att = d_att_flat.reshape(VIEWS, TOK, HEADS, head_dim)

    def backward_view(carried, view_items):
        key_sum, value_sum = carried
        view_index, query_rows, key_rows, value_rows, d_rows = view_items
        soft_weights = weights_of(query_rows, key_rows)
        rounded = lax.optimization_barrier(soft_weights.astype(jnp.bfloat16)).astype(jnp.float32)
        d_probs = jnp.einsum('qhe,khe->hqk', d_rows.astype(jnp.float32), value_rows.astype(jnp.float32))
        row_delta = lax.optimization_barrier(jnp.sum(soft_weights * d_probs, axis=-1, keepdims=True))
        d_scores = (soft_weights * (d_probs - row_delta) * score_scale).astype(jnp.bfloat16)
        d_scores = lax.optimization_barrier(d_scores).astype(jnp.float32)
        d_query = jnp.einsum('hqk,khe->qhe', d_scores, key_rows.astype(jnp.float32)).astype(jnp.bfloat16)
        d_keys = jnp.einsum('hqk,qhe->khe', d_scores, query_rows.astype(jnp.float32)).reshape(key_span, TOK, HEADS, head_dim)
        d_values = jnp.einsum('hqk,qhe->khe', rounded, d_rows.astype(jnp.float32)).reshape(key_span, TOK, HEADS, head_dim)
        for slot_index, offset in enumerate(range(-REACH, REACH + 1)):
            target = (view_index + offset) % VIEWS
            key_sum = key_sum.at[target].add(d_keys[slot_index])
            value_sum = value_sum.at[target].add(d_values[slot_index])
        return ((key_sum, value_sum), d_query)
    zeros_kv = jnp.zeros((VIEWS, TOK, HEADS, head_dim), jnp.float32)
    view_ids = jnp.arange(VIEWS, dtype=jnp.int32)
    (key_sum, value_sum), d_query_all = lax.scan(backward_view, (zeros_kv, zeros_kv), (view_ids, queries, key_all, value_all, d_att))
    d_projected = jnp.stack([d_query_all, key_sum.astype(jnp.bfloat16), value_sum.astype(jnp.bfloat16)], axis=2)
    d_projected = d_projected.reshape(TOKENS, 3 * D)
    d_input = jnp.dot(d_projected, w_flat.T, preferred_element_type=jnp.float32).astype(jnp.bfloat16)

    def weight_view(accumulated, view_items):
        rows_x, rows_dq, rows_dy, rows_att = view_items
        part_qkv = jnp.dot(rows_x.T, rows_dq, preferred_element_type=jnp.float32).reshape(D, 3, D)
        part_out = jnp.dot(rows_dy.T, rows_att, preferred_element_type=jnp.float32).reshape(D, 1, D)
        partials = jnp.concatenate([part_qkv, part_out], axis=1)
        partials = lax.optimization_barrier(partials.astype(jnp.bfloat16)).astype(jnp.float32)
        return (accumulated + partials, None)
    accumulated, unused = lax.scan(weight_view, jnp.zeros((D, 4, D), jnp.float32), (x_tokens.reshape(VIEWS, TOK, D), d_projected.reshape(VIEWS, TOK, 3 * D), grad_out.reshape(VIEWS, TOK, D), attended_flat.reshape(VIEWS, TOK, D)))
    return (mixed_out, d_input, accumulated[:, :3], accumulated[:, 3])
```

```python
import functools
import math

import jax
import jax.numpy as jnp
from jax import lax
from jax.experimental import pallas as pl
from jax.experimental.pallas import tpu as pltpu
from jax.sharding import PartitionSpec as P

D = 3072
HEADS = 24
E = 128
TOK = 512
LH = 3
LW = LH * E
ROWS = D // 16
SCALE = 1.0 / math.sqrt(E)
EXP2_SCALE = SCALE * math.log2(math.e)
BF = jnp.bfloat16
F32 = jnp.float32
VMEM_LIMIT = 56 << 20


def sds(shape, dtype):
    return jax.ShapeDtypeStruct(shape, dtype)


def dot(a, b, dims=((1,), (0,))):
    return lax.dot_general(a, b, (dims, ((), ())), preferred_element_type=F32)


def params():
    return pltpu.CompilerParams(vmem_limit_bytes=VMEM_LIMIT)


def cost(flops, moved, exps=0):
    return pl.CostEstimate(flops=int(flops), bytes_accessed=int(moved), transcendentals=int(exps))


def view_route(step):
    return [(v, step(v) % 16) for v in range(16)]


SWAP = view_route(lambda v: v ^ 1)
NEAR = view_route(lambda v: v + 2 if v % 2 == 0 else v - 2)
FAR = view_route(lambda v: v - 2 if v % 2 == 0 else v + 2)
BACK_ONE = view_route(lambda v: v - 1 if v % 2 == 0 else v + 1)


def z_route(dz):
    return [(v, (v // 8) * 8 + ((v // 2 + dz) % 4) * 2 + v % 2) for v in range(16)]


X_HI = view_route(lambda v: v + 8)
HEAD_STEPS = [(dy, dx) for dy in range(4) for dx in range(2)]


def head_route(dy, dx):
    return [(h, ((h // 2 + dy) % 4) * 2 + (h % 2 ^ dx)) for h in range(8)]


def over_view(block, route):
    return lax.ppermute(block, "view", route)


def over_head(block, step):
    return lax.ppermute(block, "head", head_route(*step))


def kv_kernel(x_ref, wk_ref, wv_ref, *refs):
    kv_refs = refs[:LH]
    acc = refs[LH]
    step = pl.program_id(0)
    x = x_ref[...]
    k = dot(x, wk_ref[...])
    v = dot(x, wv_ref[...])

    @pl.when(step == 0)
    def _():
        acc[:, :LW] = k
        acc[:, LW:] = v

    @pl.when((step > 0) & (step < 3))
    def _():
        acc[:, :LW] += k
        acc[:, LW:] += v

    @pl.when(step == 3)
    def _():
        for h in range(LH):
            cols = slice(h * E, (h + 1) * E)
            kv_refs[h][:, :E] = (acc[:, cols] + k[:, cols]).astype(BF)
            kv_refs[h][:, E:] = (acc[:, LW + h * E : LW + (h + 1) * E] + v[:, cols]).astype(BF)


def project_kv(x, w3):
    depth = D // 4
    return pl.pallas_call(
        kv_kernel,
        grid=(4,),
        in_specs=[
            pl.BlockSpec((TOK, depth), lambda i: (0, i)),
            pl.BlockSpec((None, depth, LW), lambda i: (1, i, 0)),
            pl.BlockSpec((None, depth, LW), lambda i: (2, i, 0)),
        ],
        out_specs=[pl.BlockSpec((TOK, 2 * E), lambda i: (0, 0))] * LH,
        out_shape=[sds((TOK, 2 * E), BF)] * LH,
        scratch_shapes=[pltpu.VMEM((TOK, 2 * LW), F32)],
        compiler_params=params(),
        cost_estimate=cost(2 * TOK * D * 2 * LW, 9 << 20),
    )(x, w3, w3)


def attention_kernel(q_ref, g_ref, o_ref, a_ref, b_ref, c_ref, r_ref, _x, _g, att_dq_ref, d_o, d_a, d_bc, d_r, s_scr, dp_scr):
    n = TOK
    kvs = (o_ref, a_ref, b_ref, c_ref, r_ref)
    outs = (d_o, d_a, d_bc.at[0], d_bc.at[1], d_r)
    q = q_ref[...]
    g = g_ref[...]
    q_t = q.T
    g_t = g.T
    top = None
    for j, kv in enumerate(kvs):
        s = dot(kv[:, :E], q_t)
        s_scr[j * n : (j + 1) * n] = s
        here = jnp.max(s, axis=0, keepdims=True)
        top = here if top is None else jnp.maximum(top, here)
    top = top * EXP2_SCALE
    total = None
    for j in range(5):
        e = jnp.exp2(s_scr[j * n : (j + 1) * n] * EXP2_SCALE - top)
        s_scr[j * n : (j + 1) * n] = e
        here = jnp.sum(e, axis=0, keepdims=True)
        total = here if total is None else total + here
    inverse = 1.0 / total
    delta = None
    acc = None
    for j, kv in enumerate(kvs):
        p = s_scr[j * n : (j + 1) * n] * inverse
        s_scr[j * n : (j + 1) * n] = p
        p_bf = p.astype(BF)
        v = kv[:, E:]
        dp = dot(v, g_t)
        dp_scr[j * n : (j + 1) * n] = dp
        here = jnp.sum(p * dp, axis=0, keepdims=True)
        delta = here if delta is None else delta + here
        term = dot(v.T, p_bf)
        acc = term if acc is None else acc + term
        outs[j][:, E:] = dot(p_bf, g).astype(outs[j].dtype)
    att_dq_ref[0] = acc.T.astype(BF)
    acc = None
    for j, kv in enumerate(kvs):
        ds = (s_scr[j * n : (j + 1) * n] * (dp_scr[j * n : (j + 1) * n] - delta) * SCALE).astype(BF)
        k = kv[:, :E]
        term = dot(k.T, ds)
        acc = term if acc is None else acc + term
        outs[j][:, :E] = dot(ds, q).astype(outs[j].dtype)
    att_dq_ref[1] = acc.T.astype(BF)


def attention(h, queries, d_att, kvs, before):
    head_block = pl.BlockSpec((TOK, E), lambda i: (0, h))
    pair = pl.BlockSpec((TOK, 2 * E), lambda i: (0, 0))
    return pl.pallas_call(
        attention_kernel,
        grid=(1,),
        in_specs=[head_block, head_block] + [pair] * 5 + [pl.BlockSpec(memory_space=pl.ANY)] * 2,
        out_specs=[
            pl.BlockSpec((2, TOK, E), lambda i: (0, 0, 0)),
            pair,
            pair,
            pl.BlockSpec((2, TOK, 2 * E), lambda i: (0, 0, 0)),
            pair,
        ],
        out_shape=[
            sds((2, TOK, E), BF),
            sds((TOK, 2 * E), F32),
            sds((TOK, 2 * E), BF),
            sds((2, TOK, 2 * E), BF),
            sds((TOK, 2 * E), F32),
        ],
        scratch_shapes=[pltpu.VMEM((5 * TOK, TOK), F32)] * 2,
        compiler_params=params(),
        cost_estimate=cost(6 * 2 * TOK * 5 * TOK * E * 2, 4 << 20, 5 * TOK * TOK),
    )(queries, d_att, *kvs, *before)


def rows_kernel(k_of, dest_ref, *refs):
    parts = refs[: len(k_of)]
    w_ref = refs[len(k_of)]
    outs = refs[len(k_of) + 2 : len(k_of) + 10]
    a_scr = refs[-1]

    @pl.when(pl.program_id(0) == 0)
    def _():
        for i in range(8):
            rows = pl.ds(pl.multiple_of(dest_ref[i] * 64, 64), 64)
            for part, places in zip(parts, k_of):
                piece = part[rows, :] if len(part.shape) == 2 else part[0, rows, :]
                for src, dst in places:
                    a_scr[i * 64 : (i + 1) * 64, dst : dst + E] = piece[:, src : src + E]

    a = a_scr[...]
    if len(w_ref.shape) == 2:
        out = dot(a, w_ref[...], ((1,), (1,)))
    else:
        out = None
        for i in range(w_ref.shape[0]):
            term = dot(a[:, i * LW : (i + 1) * LW], w_ref[i], ((1,), (1,)))
            out = term if out is None else out + term
    out = out.astype(BF)
    for i in range(8):
        outs[i][...] = out[i * 64 : (i + 1) * 64]


def rows_product(dest, parts, k_of, weights, tiles, before):
    cols = D // tiles
    part_specs = []
    for part in parts:
        if part.ndim == 2:
            part_specs.append(pl.BlockSpec(part.shape, lambda t, s: (0, 0)))
        else:
            part_specs.append(pl.BlockSpec((1,) + part.shape[1:], lambda t, s: (part_index[0], 0, 0)))
    part_index = [1] if weights.ndim == 3 else [0]
    if weights.ndim == 2:
        w_spec = pl.BlockSpec((cols, LW), lambda t, s: (t, 0))
        depth = LW
    else:
        w_spec = pl.BlockSpec((3, cols, LW), lambda t, s: (0, t, 0))
        depth = 3 * LW
    return pl.pallas_call(
        functools.partial(rows_kernel, k_of),
        grid_spec=pltpu.PrefetchScalarGridSpec(
            num_scalar_prefetch=1,
            grid=(tiles,),
            in_specs=part_specs + [w_spec, pl.BlockSpec(memory_space=pl.ANY)],
            out_specs=[pl.BlockSpec((64, cols), lambda t, s: (0, t))] * 8,
            scratch_shapes=[pltpu.VMEM((TOK, depth), BF)],
        ),
        out_shape=[sds((64, D), BF)] * 8,
        compiler_params=params(),
        cost_estimate=cost(2 * TOK * D * depth, (depth * D + 2 * TOK * D) * 2),
    )(dest, *parts, weights, before)


def place_kernel(src_ref, *refs):
    out_ref = refs[8]
    for i in range(8):
        rows = pl.ds(pl.multiple_of(src_ref[i] * 64, 64), 64)
        out_ref[rows, :] = refs[i][...]


def place(source, chunks):
    cols = D // 4
    return pl.pallas_call(
        place_kernel,
        grid_spec=pltpu.PrefetchScalarGridSpec(
            num_scalar_prefetch=1,
            grid=(4,),
            in_specs=[pl.BlockSpec((64, cols), lambda t, s: (0, t))] * 8,
            out_specs=pl.BlockSpec((TOK, cols), lambda t, s: (0, t)),
        ),
        out_shape=sds((TOK, D), BF),
        compiler_params=params(),
        cost_estimate=cost(0, 4 * TOK * D),
    )(source, *chunks)


def head_sum(chunks):
    got = [chunks[0]] + [over_head(chunks[i], HEAD_STEPS[i]) for i in range(1, 8)]
    total = got[0].astype(F32)
    for chunk in got[1:]:
        total = total + chunk.astype(F32)
    return total.astype(BF)


def head_gather(source, chunk):
    return place(source, [chunk] + [over_head(chunk, HEAD_STEPS[i]) for i in range(1, 8)])


def turn_kernel(core_ref, x_ref, mine_ref, other_ref, scr):
    scr[...] = x_ref[...].T
    core = core_ref[0]
    mine_ref[...] = scr[pl.ds(pl.multiple_of(core * ROWS, ROWS), ROWS), :]
    other_ref[...] = scr[pl.ds(pl.multiple_of((1 - core) * ROWS, ROWS), ROWS), :]


def turn(core, x):
    block = pl.BlockSpec((None, ROWS, TOK), lambda c, s: (c, 0, 0))
    return pl.pallas_call(
        turn_kernel,
        grid_spec=pltpu.PrefetchScalarGridSpec(
            num_scalar_prefetch=1,
            grid=(8,),
            in_specs=[pl.BlockSpec((TOK, 2 * ROWS), lambda c, s: (0, c))],
            out_specs=[block, block],
            scratch_shapes=[pltpu.VMEM((2 * ROWS, TOK), BF)],
        ),
        out_shape=[sds((8, ROWS, TOK), BF)] * 2,
        compiler_params=params(),
        cost_estimate=cost(TOK * D * 64, 4 * TOK * D),
    )(core, x)


def weight_kernel(plan, n_lhs, n_rhs, at_ref, *refs):
    lhs = refs[: 4 * n_lhs]
    rhs = refs[4 * n_lhs : 4 * n_lhs + n_rhs]
    outs = refs[4 * n_lhs + n_rhs :]
    step = pl.program_id(0)
    for i in range(4):
        @pl.when(step == i)
        def _():
            for pick, mine, theirs, dst in plan:
                top_m, low_m, top_t, low_t = lhs[4 * pick : 4 * pick + 4]
                left = jnp.concatenate([top_m[...], low_m[...]], axis=0)
                right = jnp.concatenate([top_t[...], low_t[...]], axis=0)
                out = dot(left, mine(rhs)) + dot(right, theirs(rhs))
                out = out.astype(BF)
                width = out.shape[1]
                outs[i][0, :, dst : dst + width] = out[:ROWS]
                outs[i][1, :, dst : dst + width] = out[ROWS:]


def weight_terms(at, lhs_pairs, rhs, plan):
    own = pl.BlockSpec((None, None, ROWS, TOK), lambda i, s: (s[4], s[i], 0, 0))
    far = pl.BlockSpec((None, None, ROWS, TOK), lambda i, s: (1 - s[4], s[i], 0, 0))
    lhs = []
    for mine, theirs in lhs_pairs:
        mine = mine.reshape(2, 4, ROWS, TOK)
        theirs = theirs.reshape(2, 4, ROWS, TOK)
        lhs += [mine, mine, theirs, theirs]
    rhs_specs = [
        pl.BlockSpec(r.shape, functools.partial(lambda nd, i, s: (0,) * nd, r.ndim)) for r in rhs
    ]
    out_block = pl.BlockSpec((2, ROWS, 2 * LW), lambda i, s: (0, 0, 0))
    return pl.pallas_call(
        functools.partial(weight_kernel, plan, len(lhs_pairs), len(rhs)),
        grid_spec=pltpu.PrefetchScalarGridSpec(
            num_scalar_prefetch=1,
            grid=(4,),
            in_specs=[own, far] * (2 * len(lhs_pairs)) + rhs_specs,
            out_specs=[out_block] * 4,
        ),
        out_shape=[sds((2, ROWS, 2 * LW), BF)] * 4,
        compiler_params=params(),
        cost_estimate=cost(2 * 8 * ROWS * 2 * TOK * 2 * LW, 10 << 20),
    )(at, *lhs, *rhs)


def weight_sum(terms):
    total = terms[0].astype(F32)
    for dz in range(1, 4):
        total = total + over_view(terms[dz], z_route(dz)).astype(F32)
    return total[0] + over_view(total[1].astype(BF), X_HI).astype(F32)


def local(x_tokens, w_qkv, w_out, grad_out):
    view = lax.axis_index("view")
    head = lax.axis_index("head")
    core = (view % 2).astype(jnp.int32)
    chip_z = view // 2 % 4
    x_hi = view // 8
    dest = jnp.stack([((head // 2 + dy) % 4) * 2 + (head % 2 ^ dx) for dy, dx in HEAD_STEPS]).astype(jnp.int32)
    source = jnp.stack([((head // 2 - dy) % 4) * 2 + (head % 2 ^ dx) for dy, dx in HEAD_STEPS]).astype(jnp.int32)
    at = jnp.stack([(chip_z + dz) % 4 for dz in range(4)] + [x_hi]).astype(jnp.int32)
    core = core.reshape(1)
    w3 = jnp.transpose(w_qkv, (1, 0, 2))

    own = project_kv(x_tokens, w3)
    near = [over_view(kv, NEAR) for kv in own]
    far = [over_view(kv, FAR) for kv in own]
    beside = [over_view(kv, SWAP) for kv in own]
    relayed = [over_view(kv, SWAP) for kv in far]

    queries = jnp.dot(x_tokens, w3[0], preferred_element_type=F32).astype(BF)
    d_att = jnp.dot(grad_out, w_out, preferred_element_type=F32).astype(BF)

    x_mine, x_other = turn(core, x_tokens)
    x_theirs = over_view(x_other, SWAP)
    g_mine, g_other = turn(core, grad_out)
    g_theirs = over_view(g_other, SWAP)

    att_dq = []
    d_kv = []
    for h in range(LH):
        pair, d_own, d_near, d_swap, d_relay = attention(
            h, queries, d_att, (own[h], near[h], far[h], beside[h], relayed[h]), (x_other, g_other)
        )
        att_dq.append(pair)
        back = over_view(d_swap, SWAP)
        relay = (d_relay + back[0].astype(F32)).astype(BF)
        two = over_view(d_near, FAR)
        one = over_view(relay, BACK_ONE)
        d_kv.append((d_own + back[1].astype(F32) + two.astype(F32) + one.astype(F32)).astype(BF))

    mixed_chunks = rows_product(dest, att_dq, [[(0, E * h)] for h in range(LH)], w_out, 4, relay)
    mixed_part = head_sum(mixed_chunks)

    att_dq_theirs = [over_view(pair, SWAP) for pair in att_dq]

    def joined(which, base):
        return lambda rhs: jnp.concatenate([rhs[base + h][which] for h in range(LH)], axis=1)

    early = weight_terms(
        at,
        [(x_mine, x_theirs), (g_mine, g_theirs)],
        att_dq + att_dq_theirs,
        [(0, joined(1, 0), joined(1, LH), 0), (1, joined(0, 0), joined(0, LH), LW)],
    )
    early_sum = weight_sum(early)

    d_in_chunks = rows_product(
        dest,
        att_dq + d_kv,
        [[(0, E * h)] for h in range(LH)] + [[(0, LW + E * h), (E, 2 * LW + E * h)] for h in range(LH)],
        w3,
        4,
        early[0],
    )
    d_in_part = head_sum(d_in_chunks)

    d_kv_theirs = [over_view(pair, SWAP) for pair in d_kv]

    def columns(first, base):
        return lambda rhs: jnp.concatenate([rhs[base + h][:, first : first + E] for h in range(LH)], axis=1)

    late = weight_terms(
        at,
        [(x_mine, x_theirs)],
        d_kv + d_kv_theirs,
        [(0, columns(0, 0), columns(0, LH), 0), (0, columns(E, 0), columns(E, LH), LW)],
    )
    late_sum = weight_sum(late)

    mixed_out = head_gather(source, mixed_part)
    d_input = head_gather(source, d_in_part)
    d_w = jnp.stack([early_sum[:, :LW], late_sum[:, :LW], late_sum[:, LW:]], axis=1)
    return (mixed_out, d_input, d_w, early_sum[:, LW:])


def solution(mesh):
    placed = (P("view", None), P(None, None, "head"), P(None, "head"), P("view", None))
    return jax.shard_map(
        local,
        mesh=mesh,
        in_specs=placed,
        out_specs=(P("view", None), P("view", None), P("view", None, "head"), P("view", "head")),
        check_vma=False,
    )
```

```python
import functools
import math

import jax
import jax.numpy as jnp
from jax import lax
from jax.experimental import pallas as pl
from jax.experimental.pallas import tpu as pltpu
from jax.sharding import PartitionSpec as P

D = 3072
HEADS = 24
E = 128
TOK = 512
LH = 3
LW = LH * E
ROWS = D // 16
SCALE = 1.0 / math.sqrt(E)
EXP2_SCALE = SCALE * math.log2(math.e)
BF = jnp.bfloat16
F32 = jnp.float32
VMEM_LIMIT = 56 << 20


def sds(shape, dtype):
    return jax.ShapeDtypeStruct(shape, dtype)


def dot(a, b, dims=((1,), (0,))):
    return lax.dot_general(a, b, (dims, ((), ())), preferred_element_type=F32)


def params():
    return pltpu.CompilerParams(vmem_limit_bytes=VMEM_LIMIT)


def cost(flops, moved, exps=0):
    return pl.CostEstimate(flops=int(flops), bytes_accessed=int(moved), transcendentals=int(exps))


def view_route(step):
    return [(v, step(v) % 16) for v in range(16)]


SWAP = view_route(lambda v: v ^ 1)
NEAR = view_route(lambda v: v + 2 if v % 2 == 0 else v - 2)
FAR = view_route(lambda v: v - 2 if v % 2 == 0 else v + 2)


BACK_ONE = view_route(lambda v: v - 1 if v % 2 == 0 else v + 1)
HEAD_STEPS = [(dy, dx) for dx in range(2) for dy in range(4)]
HALF = D // 2
X_LO = (0, 1)


def head_route(dy, dx):
    return [(h, ((h // 2 + dy) % 4) * 2 + (h % 2 ^ dx)) for h in range(8)]


def over_view(block, route):
    return lax.ppermute(block, "view", route)


def over_head(block, step):
    return lax.ppermute(block, "head", head_route(*step))


def kv_kernel(x_ref, wk_ref, wv_ref, kv_ref, acc):
    step = pl.program_id(0)
    x = x_ref[...]
    k = dot(x, wk_ref[...])
    v = dot(x, wv_ref[...])

    @pl.when(step == 0)
    def _():
        acc[:, :LW] = k
        acc[:, LW:] = v

    @pl.when((step > 0) & (step < 3))
    def _():
        acc[:, :LW] += k
        acc[:, LW:] += v

    @pl.when(step == 3)
    def _():
        for h in range(LH):
            cols = slice(h * E, (h + 1) * E)
            kv_ref[h, :, :E] = (acc[:, cols] + k[:, cols]).astype(BF)
            kv_ref[h, :, E:] = (acc[:, LW + h * E : LW + (h + 1) * E] + v[:, cols]).astype(BF)


def project_kv(x, w3):
    depth = D // 4
    return pl.pallas_call(
        kv_kernel,
        grid=(4,),
        in_specs=[
            pl.BlockSpec((TOK, depth), lambda i: (0, i)),
            pl.BlockSpec((None, depth, LW), lambda i: (1, i, 0)),
            pl.BlockSpec((None, depth, LW), lambda i: (2, i, 0)),
        ],
        out_specs=pl.BlockSpec((LH, TOK, 2 * E), lambda i: (0, 0, 0)),
        out_shape=sds((LH, TOK, 2 * E), BF),
        scratch_shapes=[pltpu.VMEM((TOK, 2 * LW), F32)],
        compiler_params=params(),
        cost_estimate=cost(2 * TOK * D * 2 * LW, 9 << 20),
    )(x, w3, w3)


def attention_kernel(q_ref, g_ref, o_ref, a_ref, b_ref, c_ref, r_ref, *refs):
    att_dq_ref, d_o, d_a, d_bc, d_r, s_scr, dp_scr = refs[-7:]
    n = TOK
    kvs = (o_ref, a_ref, b_ref, c_ref, r_ref)
    outs = (d_o, d_a, d_bc.at[0], d_bc.at[1], d_r)
    q = q_ref[...]
    g = g_ref[...]
    q_t = q.T
    g_t = g.T
    top = None
    for j, kv in enumerate(kvs):
        s = dot(kv[:, :E], q_t)
        s_scr[j * n : (j + 1) * n] = s
        here = jnp.max(s, axis=0, keepdims=True)
        top = here if top is None else jnp.maximum(top, here)
    top = top * EXP2_SCALE
    total = None
    for j in range(5):
        e = jnp.exp2(s_scr[j * n : (j + 1) * n] * EXP2_SCALE - top)
        s_scr[j * n : (j + 1) * n] = e
        here = jnp.sum(e, axis=0, keepdims=True)
        total = here if total is None else total + here
    inverse = 1.0 / total
    delta = None
    acc = None
    for j, kv in enumerate(kvs):
        p = s_scr[j * n : (j + 1) * n] * inverse
        s_scr[j * n : (j + 1) * n] = p
        p_bf = p.astype(BF)
        v = kv[:, E:]
        dp = dot(v, g_t)
        dp_scr[j * n : (j + 1) * n] = dp
        here = jnp.sum(p * dp, axis=0, keepdims=True)
        delta = here if delta is None else delta + here
        term = dot(v.T, p_bf)
        acc = term if acc is None else acc + term
        outs[j][:, E:] = dot(p_bf, g).astype(outs[j].dtype)
    att_dq_ref[0] = acc.T.astype(BF)
    acc = None
    for j, kv in enumerate(kvs):
        ds = (s_scr[j * n : (j + 1) * n] * (dp_scr[j * n : (j + 1) * n] - delta) * SCALE).astype(BF)
        k = kv[:, :E]
        term = dot(k.T, ds)
        acc = term if acc is None else acc + term
        outs[j][:, :E] = dot(ds, q).astype(outs[j].dtype)
    att_dq_ref[1] = acc.T.astype(BF)


def attention(queries, d_att, kvs):
    head_block = pl.BlockSpec((TOK, E), lambda h: (0, h))
    pair = pl.BlockSpec((None, TOK, 2 * E), lambda h: (h, 0, 0))
    return pl.pallas_call(
        attention_kernel,
        grid=(LH,),
        in_specs=[head_block, head_block] + [pair] * 5,
        out_specs=[
            pl.BlockSpec((2, TOK, E), lambda h: (0, 0, h)),
            pair,
            pair,
            pl.BlockSpec((2, None, TOK, 2 * E), lambda h: (0, h, 0, 0)),
            pair,
        ],
        out_shape=[
            sds((2, TOK, LW), BF),
            sds((LH, TOK, 2 * E), F32),
            sds((LH, TOK, 2 * E), BF),
            sds((2, LH, TOK, 2 * E), BF),
            sds((LH, TOK, 2 * E), F32),
        ],
        scratch_shapes=[pltpu.VMEM((5 * TOK, TOK), F32)] * 2,
        compiler_params=params(),
        cost_estimate=cost(LH * 6 * 2 * TOK * 5 * TOK * E * 2, 12 << 20, LH * 5 * TOK * TOK),
    )(queries, d_att, *kvs)


COLS = D // 4


def left_tile(rows):
    return pl.BlockSpec((rows, COLS), lambda t, *s: (0, jnp.minimum(t, 1)))


def right_tile(rows):
    return pl.BlockSpec((rows, COLS), lambda t, *s: (0, jnp.maximum(t - 2, 0)))


def gather_rows(dest_ref, a_scr, pieces):
    for i in range(8):
        rows = pl.ds(pl.multiple_of(dest_ref[i] * 64, 64), 64)
        for at, part in pieces:
            a_scr[i * 64 : (i + 1) * 64, at : at + part.shape[1]] = part[rows, :]


def y_rows(out, dy):
    return out[dy * 64 : (dy + 1) * 64], out[256 + dy * 64 : 256 + (dy + 1) * 64]


def mixed_kernel(dest_ref, att_ref, w_ref, near_ref, far_ref, y0_ref, y1_ref, y2_ref, y3_ref, a_scr):
    tile = pl.program_id(0)

    @pl.when(tile == 0)
    def _():
        gather_rows(dest_ref, a_scr, [(0, att_ref)])

    out = dot(a_scr[...], w_ref[...], ((1,), (1,))).astype(BF)

    @pl.when(tile < 2)
    def _():
        near_ref[...] = out[:256]
        far_ref[...] = out[256:]

    @pl.when(tile >= 2)
    def _():
        for dy, ref in enumerate((y0_ref, y1_ref, y2_ref, y3_ref)):
            ref[:64], ref[64:] = y_rows(out, dy)


def mixed_product(dest, att_dq, w_out):
    return pl.pallas_call(
        mixed_kernel,
        grid_spec=pltpu.PrefetchScalarGridSpec(
            num_scalar_prefetch=1,
            grid=(4,),
            in_specs=[
                pl.BlockSpec((None, TOK, LW), lambda t, s: (0, 0, 0)),
                pl.BlockSpec((COLS, LW), lambda t, s: (t, 0)),
            ],
            out_specs=[left_tile(256)] * 2 + [right_tile(128)] * 4,
            scratch_shapes=[pltpu.VMEM((TOK, LW), BF)],
        ),
        out_shape=[sds((256, HALF), BF)] * 2 + [sds((128, HALF), BF)] * 4,
        compiler_params=params(),
        cost_estimate=cost(2 * TOK * D * LW, (LW * D + TOK * D) * 2),
    )(dest, att_dq, w_out)


def input_kernel(dest_ref, *refs):
    dq_ref, d_kv_ref, w_ref, near_in, far_in, y0_in, y1_in, y2_in, y3_in = refs[:9]
    near_ref, y0_ref, left_ref, right_ref, x_ref, y1_ref, y2_ref, y3_ref, a_scr = refs[9:]
    tile = pl.program_id(0)

    @pl.when(tile == 0)
    def _():
        pieces = [(0, dq_ref)]
        for h in range(LH):
            pieces += [(LW + E * h, d_kv_ref.at[h, :, :E]), (2 * LW + E * h, d_kv_ref.at[h, :, E:])]
        gather_rows(dest_ref, a_scr, pieces)

    a = a_scr[...]
    out = None
    for i in range(3):
        term = dot(a[:, i * LW : (i + 1) * LW], w_ref[i], ((1,), (1,)))
        out = term if out is None else out + term
    out = out.astype(BF)

    @pl.when(tile < 2)
    def _():
        near_ref[...] = out[:256]
        x_ref[:256] = out[256:]
        total = y0_in[...].astype(F32)
        for ref in (y1_in, y2_in, y3_in):
            total = total + ref[...].astype(F32)
        right_ref[...] = total[:64]
        x_ref[256:] = total[64:].astype(BF)

    @pl.when(tile >= 2)
    def _():
        total = near_in[...].astype(F32) + far_in[...].astype(F32)
        left_ref[...] = total[:64]
        y0_ref[:64], y0_ref[64:] = y_rows(out, 0)
        for dy, ref in ((1, y1_ref), (2, y2_ref), (3, y3_ref)):
            ref[:64], ref[64:128] = y_rows(out, dy)
            ref[128:] = total[dy * 64 : (dy + 1) * 64].astype(BF)


def input_product(dest, att_dq, d_kv, w3, mixed):
    return pl.pallas_call(
        input_kernel,
        grid_spec=pltpu.PrefetchScalarGridSpec(
            num_scalar_prefetch=1,
            grid=(4,),
            in_specs=[
                pl.BlockSpec((None, TOK, LW), lambda t, s: (1, 0, 0)),
                pl.BlockSpec((LH, TOK, 2 * E), lambda t, s: (0, 0, 0)),
                pl.BlockSpec((3, COLS, LW), lambda t, s: (0, t, 0)),
            ]
            + [right_tile(256)] * 2
            + [left_tile(128)] * 4,
            out_specs=[left_tile(256), right_tile(128), right_tile(64), left_tile(64), left_tile(320)]
            + [right_tile(192)] * 3,
            scratch_shapes=[pltpu.VMEM((TOK, 3 * LW), BF)],
        ),
        out_shape=[
            sds((256, HALF), BF),
            sds((128, HALF), BF),
            sds((64, HALF), F32),
            sds((64, HALF), F32),
            sds((320, HALF), BF),
        ]
        + [sds((192, HALF), BF)] * 3,
        compiler_params=params(),
        cost_estimate=cost(2 * TOK * D * 3 * LW, (3 * LW * D + 2 * TOK * D) * 2),
    )(dest, att_dq, d_kv, w3, *mixed)


def third_kernel(near_in, y0_in, left_in, right_in, x_in, y1_in, y2_in, y3_in, *refs):
    left_ref, right_ref, x_ref, y1_ref, y2_ref, y3_ref = refs
    y_in = (y1_in, y2_in, y3_in)
    mixed_left = left_in[...]
    for ref in y_in:
        mixed_left = mixed_left + ref[128:].astype(F32)
    mixed_left = mixed_left.astype(BF)
    x_ref[64:] = (right_in[...] + x_in[256:].astype(F32)).astype(BF)
    total = near_in[...].astype(F32) + x_in[:256].astype(F32)
    left_ref[...] = total[:64]
    for dy, ref in ((1, y1_ref), (2, y2_ref), (3, y3_ref)):
        ref[:64] = total[dy * 64 : (dy + 1) * 64].astype(BF)
        ref[64:] = mixed_left
    total = y0_in[...].astype(F32)
    for ref in y_in:
        total = total + ref[:128].astype(F32)
    right_ref[...] = total[:64]
    x_ref[:64] = total[64:].astype(BF)


def fourth_kernel(left_in, right_in, x_own, x_in, y_own, y1_in, y2_in, y3_in, x_ref, y_ref):
    y_in = (y1_in, y2_in, y3_in)
    left = left_in[...]
    for ref in y_in:
        left = left + ref[:64].astype(F32)
    y_ref[:64] = left.astype(BF)
    y_ref[64:128] = x_own[64:]
    y_ref[128:] = x_in[64:]
    x_ref[:64] = (right_in[...] + x_in[:64].astype(F32)).astype(BF)
    x_ref[64:128] = y_own[64:]
    for dy, ref in enumerate(y_in):
        x_ref[128 + dy * 64 : 192 + dy * 64] = ref[64:]


def fifth_kernel(x_own, x_in, y_own, y1_in, y2_in, y3_in, x_ref, y_ref):
    x_ref[:64] = y_own[:64]
    for dy, ref in enumerate((y1_in, y2_in, y3_in)):
        x_ref[64 + dy * 64 : 128 + dy * 64] = ref[:64]
    y_ref[:64] = x_own[:64]
    y_ref[64:] = x_in[:64]


def by_columns(kernel, inputs, outputs):
    def tile(rows):
        return pl.BlockSpec((rows, COLS), lambda t: (0, t))

    return pl.pallas_call(
        kernel,
        grid=(2,),
        in_specs=[tile(a.shape[0]) for a in inputs],
        out_specs=[tile(rows) for rows, _ in outputs],
        out_shape=[sds((rows, HALF), dtype) for rows, dtype in outputs],
        compiler_params=params(),
        cost_estimate=cost(5e10, 4 << 20),
    )(*inputs)


def exchange(x, ys):
    return over_head(x, X_LO), [over_head(y, (dy, 0)) for dy, y in zip((1, 2, 3), ys)]


def place_kernel(first, src_ref, own_ref, beside_ref, y0_ref, y1_ref, y2_ref, y3_ref, out_ref):
    half = pl.program_id(0)

    def rows(i):
        return pl.ds(pl.multiple_of(src_ref[i] * 64, 64), 64)

    @pl.when(half == 0)
    def _():
        for dy, ref in enumerate((y0_ref, y1_ref, y2_ref, y3_ref)):
            out_ref[rows(dy), :] = ref[first : first + 64]
            out_ref[rows(4 + dy), :] = ref[first + 64 : first + 128]

    @pl.when(half == 1)
    def _():
        for dy in range(4):
            out_ref[rows(dy), :] = own_ref[first + dy * 64 : first + (dy + 1) * 64]
            out_ref[rows(4 + dy), :] = beside_ref[first + dy * 64 : first + (dy + 1) * 64]


def place(source, first, own, beside, ys):
    def whole(rows):
        return pl.BlockSpec((rows, HALF), lambda t, s: (0, 0))

    return pl.pallas_call(
        functools.partial(place_kernel, first),
        grid_spec=pltpu.PrefetchScalarGridSpec(
            num_scalar_prefetch=1,
            grid=(2,),
            in_specs=[whole(first + 256)] * 2 + [whole(first + 128)] * 4,
            out_specs=pl.BlockSpec((TOK, HALF), lambda t, s: (0, 1 - t)),
        ),
        out_shape=sds((TOK, D), BF),
        compiler_params=params(),
        cost_estimate=cost(5e10, 4 * TOK * D),
    )(source, own, beside, *ys)


def turn_kernel(core_ref, x_ref, _, mine_ref, other_ref, scr):
    scr[...] = x_ref[...].T
    core = core_ref[0]
    for c in range(4):
        first = c * 2 * ROWS
        mine_ref[c] = scr[pl.ds(pl.multiple_of(first + core * ROWS, ROWS), ROWS), :]
        other_ref[c] = scr[pl.ds(pl.multiple_of(first + (1 - core) * ROWS, ROWS), ROWS), :]


def turn(core, x, before):
    block = pl.BlockSpec((4, ROWS, TOK), lambda c, s: (c, 0, 0))
    return pl.pallas_call(
        turn_kernel,
        grid_spec=pltpu.PrefetchScalarGridSpec(
            num_scalar_prefetch=1,
            grid=(2,),
            in_specs=[pl.BlockSpec((TOK, HALF), lambda c, s: (0, c)), pl.BlockSpec(memory_space=pl.ANY)],
            out_specs=[block, block],
            scratch_shapes=[pltpu.VMEM((HALF, TOK), BF)],
        ),
        out_shape=[sds((8, ROWS, TOK), BF)] * 2,
        compiler_params=params(),
        cost_estimate=cost(TOK * D * 64, 4 * TOK * D),
    )(core, x, before)


def weight_kernel(plan, n_lhs, n_rhs, *refs):
    lhs = refs[: 2 * n_lhs]
    rhs = refs[2 * n_lhs : 2 * n_lhs + n_rhs]
    out_ref = refs[-1]
    for pick, mine, theirs, dst in plan:
        left, right = (
            jnp.concatenate([ref[x_hi, z] for z in range(2) for x_hi in range(2)], axis=0)
            for ref in lhs[2 * pick : 2 * pick + 2]
        )
        out = dot(left, mine(rhs)) + dot(right, theirs(rhs))
        out_ref[:, dst : dst + out.shape[1]] = out.astype(BF)


def weight_terms(lhs_pairs, rhs, plan):
    lhs = [side.reshape(2, 4, ROWS, TOK) for pair in lhs_pairs for side in pair]
    rhs_specs = [pl.BlockSpec(r.shape, functools.partial(lambda nd, i: (0,) * nd, r.ndim)) for r in rhs]
    return pl.pallas_call(
        functools.partial(weight_kernel, plan, len(lhs_pairs), len(rhs)),
        grid=(2,),
        in_specs=[pl.BlockSpec((2, 2, ROWS, TOK), lambda i: (0, i, 0, 0))] * len(lhs) + rhs_specs,
        out_specs=pl.BlockSpec((4 * ROWS, 2 * LW), lambda i: (i, 0)),
        out_shape=sds((8 * ROWS, 2 * LW), BF),
        compiler_params=params(),
        cost_estimate=cost(2 * 8 * ROWS * 2 * TOK * 2 * LW, 10 << 20),
    )(*lhs, *rhs)


Z_GROUPS = [[x_hi * 8 + z * 2 + core for z in range(4)] for x_hi in range(2) for core in range(2)]
X_HI = view_route(lambda v: v + 8)


def weight_sum(x_hi, terms):
    total = lax.psum_scatter(terms, "view", scatter_dimension=0, axis_index_groups=Z_GROUPS, tiled=True)
    own = lax.dynamic_slice_in_dim(total, x_hi * ROWS, ROWS)
    other = lax.dynamic_slice_in_dim(total, (1 - x_hi) * ROWS, ROWS)
    return own, other


def with_x_hi(own, other):
    return own.astype(F32) + over_view(other, X_HI).astype(F32)


def local(x_tokens, w_qkv, w_out, grad_out):
    view = lax.axis_index("view")
    head = lax.axis_index("head")
    core = (view % 2).astype(jnp.int32)
    dest = jnp.stack([((head // 2 + dy) % 4) * 2 + (head % 2 ^ dx) for dy, dx in HEAD_STEPS]).astype(jnp.int32)
    source = jnp.stack([((head // 2 - dy) % 4) * 2 + (head % 2 ^ dx) for dy, dx in HEAD_STEPS]).astype(jnp.int32)
    core = core.reshape(1)
    w3 = jnp.transpose(w_qkv, (1, 0, 2))

    own = project_kv(x_tokens, w3)
    far = over_view(own, FAR)
    near = over_view(own, NEAR)
    beside = over_view(own, SWAP)

    queries = jnp.dot(x_tokens, w3[0], preferred_element_type=F32).astype(BF)
    d_att = jnp.dot(grad_out, w_out, preferred_element_type=F32).astype(BF)
    x_mine, x_other = turn(core, x_tokens, d_att)
    far, near, queries, d_att, x_mine, x_other = lax.optimization_barrier(
        (far, near, queries, d_att, x_mine, x_other)
    )
    relayed = over_view(far, SWAP)

    att_dq, d_own, d_near, d_swap, d_relay = attention(queries, d_att, (own, near, far, beside, relayed))

    back = over_view(d_swap, SWAP)
    mixed_near, mixed_far, mixed_y0, *mixed_y = mixed_product(dest, att_dq, w_out)
    mixed_x, mixed_y = exchange(mixed_far, mixed_y)

    relay = (d_relay + back[0].astype(F32)).astype(BF)
    two = over_view(d_near, FAR)
    one = over_view(relay, BACK_ONE)
    d_kv = (d_own + back[1].astype(F32) + two.astype(F32) + one.astype(F32)).astype(BF)

    near2, y02, left2, right2, x2, *y2 = input_product(
        dest, att_dq, d_kv, w3, (mixed_near, mixed_x, mixed_y0, *mixed_y)
    )
    from_x2, from_y2 = exchange(x2, y2)

    x_other, _ = lax.optimization_barrier((x_other, x2))
    x_theirs = over_view(x_other, SWAP)
    g_mine, g_other = turn(core, grad_out, x2)
    g_theirs = over_view(g_other, SWAP)
    att_dq_late, _ = lax.optimization_barrier((att_dq, x2))
    att_dq_theirs = over_view(att_dq_late, SWAP)
    early = weight_terms(
        [(x_mine, x_theirs), (g_mine, g_theirs)],
        [att_dq, att_dq_theirs],
        [(0, lambda r: r[0][1], lambda r: r[1][1], 0), (1, lambda r: r[0][0], lambda r: r[1][0], LW)],
    )
    early_own, early_other = weight_sum(view // 8, early)

    d_kv_late, _ = lax.optimization_barrier((d_kv, x2))
    d_kv_theirs = over_view(d_kv_late, SWAP)

    def columns(which, first):
        return lambda r: jnp.concatenate([r[which][h, :, first : first + E] for h in range(LH)], axis=1)

    late = weight_terms(
        [(x_mine, x_theirs)],
        [d_kv_late, d_kv_theirs],
        [(0, columns(0, 0), columns(1, 0), 0), (0, columns(0, E), columns(1, E), LW)],
    )
    late_sum = with_x_hi(*weight_sum(view // 8, late))

    near2, _, _ = lax.optimization_barrier((near2, late, g_mine))
    left3, right3, x3, *y3 = by_columns(
        third_kernel,
        (near2, y02, left2, right2, from_x2, *from_y2),
        [(64, F32), (64, F32), (128, BF), (128, BF), (128, BF), (128, BF)],
    )
    from_x3, from_y3 = exchange(x3, y3)
    left3, _ = lax.optimization_barrier((left3, early))
    x4, y4 = by_columns(
        fourth_kernel, (left3, right3, x3, from_x3, y3[0], *from_y3), [(320, BF), (192, BF)]
    )
    from_x4, from_y4 = exchange(x4, [y4] * 3)
    x4, late_sum = lax.optimization_barrier((x4, late_sum))
    x5, y5 = by_columns(fifth_kernel, (x4, from_x4, y4, *from_y4), [(256, BF), (128, BF)])
    early_other, _ = lax.optimization_barrier((early_other, x5))
    early_sum = with_x_hi(early_own, early_other)
    from_x5, from_y5 = exchange(x5, [y5] * 3)
    mixed_out = place(source, 64, x4, from_x4, (y4, *from_y4))
    d_input = place(source, 0, x5, from_x5, (y5, *from_y5))

    d_w = jnp.stack([early_sum[:, :LW], late_sum[:, :LW], late_sum[:, LW:]], axis=1)
    return (mixed_out, d_input, d_w, early_sum[:, LW:])


def solution(mesh):
    placed = (P("view", None), P(None, None, "head"), P(None, "head"), P("view", None))
    return jax.shard_map(
        local,
        mesh=mesh,
        in_specs=placed,
        out_specs=(P("view", None), P("view", None), P("view", None, "head"), P("view", "head")),
        check_vma=False,
    )
```

```python
import functools
import math

import jax
import jax.numpy as jnp
from jax import lax
from jax.experimental import pallas as pl
from jax.experimental.pallas import tpu as pltpu
from jax.sharding import PartitionSpec as P

D = 3072
HEADS = 24
E = 128
TOK = 512
LH = 3
LW = LH * E
ROWS = D // 16
SCALE = 1.0 / math.sqrt(E)
EXP2_SCALE = SCALE * math.log2(math.e)
BF = jnp.bfloat16
F32 = jnp.float32


def sds(shape, dtype):
    return jax.ShapeDtypeStruct(shape, dtype)


def dot(a, b, dims=((1,), (0,))):
    return lax.dot_general(a, b, (dims, ((), ())), preferred_element_type=F32)


def params(mib=56):
    return pltpu.CompilerParams(vmem_limit_bytes=mib << 20)


def cost(flops, moved, exps=0):
    return pl.CostEstimate(flops=int(flops), bytes_accessed=int(moved), transcendentals=int(exps))


def view_route(step):
    return [(v, step(v) % 16) for v in range(16)]


SWAP = view_route(lambda v: v ^ 1)
NEAR = view_route(lambda v: v + 2 if v % 2 == 0 else v - 2)
FAR = view_route(lambda v: v - 2 if v % 2 == 0 else v + 2)


BACK_ONE = view_route(lambda v: v - 1 if v % 2 == 0 else v + 1)
HEAD_STEPS = [(dy, dx) for dx in range(2) for dy in range(4)]
HALF = D // 2
X_LO = (0, 1)


def head_route(dy, dx):
    return [(h, ((h // 2 + dy) % 4) * 2 + (h % 2 ^ dx)) for h in range(8)]


def over_view(block, route):
    return lax.ppermute(block, "view", route)


def over_head(block, step):
    return lax.ppermute(block, "head", head_route(*step))


def kv_kernel(x_ref, wk_ref, wv_ref, kv_ref, acc):
    step = pl.program_id(0)
    x = x_ref[...]
    k = dot(x, wk_ref[...])
    v = dot(x, wv_ref[...])

    @pl.when(step == 0)
    def _():
        acc[:, :LW] = k
        acc[:, LW:] = v

    @pl.when(step == 1)
    def _():
        for h in range(LH):
            cols = slice(h * E, (h + 1) * E)
            kv_ref[h, :, :E] = (acc[:, cols] + k[:, cols]).astype(BF)
            kv_ref[h, :, E:] = (acc[:, LW + h * E : LW + (h + 1) * E] + v[:, cols]).astype(BF)


def project_kv(x, w3):
    depth = D // 2
    return pl.pallas_call(
        kv_kernel,
        grid=(2,),
        in_specs=[
            pl.BlockSpec((TOK, depth), lambda i: (0, i)),
            pl.BlockSpec((None, depth, LW), lambda i: (1, i, 0)),
            pl.BlockSpec((None, depth, LW), lambda i: (2, i, 0)),
        ],
        out_specs=pl.BlockSpec((LH, TOK, 2 * E), lambda i: (0, 0, 0)),
        out_shape=sds((LH, TOK, 2 * E), BF),
        scratch_shapes=[pltpu.VMEM((TOK, 2 * LW), F32)],
        compiler_params=params(),
        cost_estimate=cost(2 * TOK * D * 2 * LW, 9 << 20),
    )(x, w3, w3)


def attention_kernel(q_ref, g_ref, o_ref, a_ref, b_ref, c_ref, r_ref, *refs):
    att_dq_ref, d_o, d_a, d_bc, d_r, s_scr, dp_scr = refs[-7:]
    n = TOK
    kvs = (o_ref, a_ref, b_ref, c_ref, r_ref)
    outs = (d_o, d_a, d_bc.at[0], d_bc.at[1], d_r)
    q = q_ref[...]
    g = g_ref[...]
    q_t = q.T
    g_t = g.T
    top = None
    for j, kv in enumerate(kvs):
        s = dot(kv[:, :E], q_t)
        s_scr[j * n : (j + 1) * n] = s
        here = jnp.max(s, axis=0, keepdims=True)
        top = here if top is None else jnp.maximum(top, here)
    top = top * EXP2_SCALE
    total = None
    for j in range(5):
        e = jnp.exp2(s_scr[j * n : (j + 1) * n] * EXP2_SCALE - top)
        s_scr[j * n : (j + 1) * n] = e
        here = jnp.sum(e, axis=0, keepdims=True)
        total = here if total is None else total + here
    inverse = 1.0 / total
    delta = None
    acc = None
    for j, kv in enumerate(kvs):
        p = s_scr[j * n : (j + 1) * n] * inverse
        s_scr[j * n : (j + 1) * n] = p
        p_bf = p.astype(BF)
        v = kv[:, E:]
        dp = dot(v, g_t)
        dp_scr[j * n : (j + 1) * n] = dp
        here = jnp.sum(p * dp, axis=0, keepdims=True)
        delta = here if delta is None else delta + here
        term = dot(v.T, p_bf)
        acc = term if acc is None else acc + term
        outs[j][:, E:] = dot(p_bf, g).astype(outs[j].dtype)
    att_dq_ref[0] = acc.T.astype(BF)
    acc = None
    for j, kv in enumerate(kvs):
        ds = (s_scr[j * n : (j + 1) * n] * (dp_scr[j * n : (j + 1) * n] - delta) * SCALE).astype(BF)
        k = kv[:, :E]
        term = dot(k.T, ds)
        acc = term if acc is None else acc + term
        outs[j][:, :E] = dot(ds, q).astype(outs[j].dtype)
    att_dq_ref[1] = acc.T.astype(BF)


def attention(queries, d_att, kvs):
    head_block = pl.BlockSpec((TOK, E), lambda h: (0, h))
    pair = pl.BlockSpec((None, TOK, 2 * E), lambda h: (h, 0, 0))
    return pl.pallas_call(
        attention_kernel,
        grid=(LH,),
        in_specs=[head_block, head_block] + [pair] * 5,
        out_specs=[
            pl.BlockSpec((2, TOK, E), lambda h: (0, 0, h)),
            pair,
            pair,
            pl.BlockSpec((2, None, TOK, 2 * E), lambda h: (0, h, 0, 0)),
            pair,
        ],
        out_shape=[
            sds((2, TOK, LW), BF),
            sds((LH, TOK, 2 * E), F32),
            sds((LH, TOK, 2 * E), BF),
            sds((2, LH, TOK, 2 * E), BF),
            sds((LH, TOK, 2 * E), F32),
        ],
        scratch_shapes=[pltpu.VMEM((5 * TOK, TOK), F32)] * 2,
        compiler_params=params(),
        cost_estimate=cost(LH * 6 * 2 * TOK * 5 * TOK * E * 2, 12 << 20, LH * 5 * TOK * TOK),
    )(queries, d_att, *kvs)


COLS = D // 4


def left_tile(rows):
    return pl.BlockSpec((rows, COLS), lambda t, *s: (0, jnp.minimum(t, 1)))


def right_tile(rows):
    return pl.BlockSpec((rows, COLS), lambda t, *s: (0, jnp.maximum(t - 2, 0)))


def gather_rows(dest_ref, a_scr, pieces):
    for i in range(8):
        rows = pl.ds(pl.multiple_of(dest_ref[i] * 64, 64), 64)
        for at, part in pieces:
            a_scr[i * 64 : (i + 1) * 64, at : at + part.shape[1]] = part[rows, :]


def y_rows(out, dy):
    return out[dy * 64 : (dy + 1) * 64], out[256 + dy * 64 : 256 + (dy + 1) * 64]


def mixed_kernel(dest_ref, att_ref, w_ref, near_ref, far_ref, y0_ref, y1_ref, y2_ref, y3_ref, a_scr):
    tile = pl.program_id(0)

    @pl.when(tile == 0)
    def _():
        gather_rows(dest_ref, a_scr, [(0, att_ref)])

    out = dot(a_scr[...], w_ref[...], ((1,), (1,))).astype(BF)

    @pl.when(tile == 0)
    def _():
        near_ref[...] = out[:256]
        far_ref[...] = out[256:]

    @pl.when(tile > 0)
    def _():
        for dy, ref in enumerate((y0_ref, y1_ref, y2_ref, y3_ref)):
            ref[:64], ref[64:] = y_rows(out, dy)


def mixed_product(dest, att_dq, w_out):
    return pl.pallas_call(
        mixed_kernel,
        grid_spec=pltpu.PrefetchScalarGridSpec(
            num_scalar_prefetch=1,
            grid=(4,),
            in_specs=[
                pl.BlockSpec((None, TOK, LW), lambda t, s: (0, 0, 0)),
                pl.BlockSpec((COLS, LW), lambda t, s: (t, 0)),
            ],
            out_specs=[pl.BlockSpec((256, COLS), lambda t, s: (0, 0))] * 2
            + [pl.BlockSpec((128, COLS), lambda t, s: (0, jnp.maximum(t - 1, 0)))] * 4,
            scratch_shapes=[pltpu.VMEM((TOK, LW), BF)],
        ),
        out_shape=[sds((256, COLS), BF)] * 2 + [sds((128, 3 * COLS), BF)] * 4,
        compiler_params=params(24),
        cost_estimate=cost(2 * TOK * D * LW, (LW * D + TOK * D) * 2),
    )(dest, att_dq, w_out)


def input_kernel(dest_ref, *refs):
    dq_ref, d_kv_ref, w_ref, near_in, far_in = refs[:5]
    y_in, y_last = refs[5:9], refs[9:13]
    near_ref, y0_ref, left_ref, right_ref, x_ref, y1_ref, y2_ref, y3_ref, a_scr = refs[13:]
    tile = pl.program_id(0)

    @pl.when(tile == 0)
    def _():
        pieces = [(0, dq_ref)]
        for h in range(LH):
            pieces += [(LW + E * h, d_kv_ref.at[h, :, :E]), (2 * LW + E * h, d_kv_ref.at[h, :, E:])]
        gather_rows(dest_ref, a_scr, pieces)

    a = a_scr[...]
    out = None
    for i in range(3):
        term = dot(a[:, i * LW : (i + 1) * LW], w_ref[i], ((1,), (1,)))
        out = term if out is None else out + term
    out = out.astype(BF)

    def total_of(parts, rows):
        total = parts[0][rows, :].astype(F32)
        for ref in parts[1:]:
            total = total + ref[rows, :].astype(F32)
        return total

    @pl.when(tile < 2)
    def _():
        near_ref[...] = out[:256]
        x_ref[:256] = out[256:]
        total = total_of(y_in, slice(0, 128))
        right_ref[...] = total[:64]
        x_ref[256:320] = total[64:].astype(BF)

    for t in range(2):
        @pl.when(tile == t)
        def _():
            x_ref[320:] = total_of(y_last, slice(64 + 32 * t, 96 + 32 * t)).astype(BF)

    @pl.when(tile == 2)
    def _():
        right_ref[...] = total_of(y_last, slice(0, 64))

    for t in range(2):
        @pl.when(tile == 2 + t)
        def _():
            total = near_in[...].astype(F32) + far_in[...].astype(F32)
            left_ref[...] = total[:64]
            y0_ref[:64], y0_ref[64:] = y_rows(out, 0)
            for dy, ref in ((1, y1_ref), (2, y2_ref), (3, y3_ref)):
                ref[:64], ref[64:128] = y_rows(out, dy)
                ref[128:] = total[dy * 64 + 32 * t : dy * 64 + 32 * t + 32].astype(BF)


def input_product(dest, att_dq, d_kv, w3, mixed):
    return pl.pallas_call(
        input_kernel,
        grid_spec=pltpu.PrefetchScalarGridSpec(
            num_scalar_prefetch=1,
            grid=(4,),
            in_specs=[
                pl.BlockSpec((None, TOK, LW), lambda t, s: (1, 0, 0)),
                pl.BlockSpec((LH, TOK, 2 * E), lambda t, s: (0, 0, 0)),
                pl.BlockSpec((3, COLS, LW), lambda t, s: (0, t, 0)),
            ]
            + [pl.BlockSpec((256, COLS), lambda t, s: (0, 0))] * 2
            + [left_tile(128)] * 4
            + [pl.BlockSpec((128, COLS), lambda t, s: (0, 2))] * 4,
            out_specs=[
                left_tile(256),
                right_tile(128),
                pl.BlockSpec((64, COLS), lambda t, s: (0, 0)),
                pl.BlockSpec((64, COLS), lambda t, s: (0, jnp.minimum(t, 2))),
                left_tile(352),
            ]
            + [right_tile(160)] * 3,
            scratch_shapes=[pltpu.VMEM((TOK, 3 * LW), BF)],
        ),
        out_shape=[
            sds((256, HALF), BF),
            sds((128, HALF), BF),
            sds((64, COLS), F32),
            sds((64, 3 * COLS), F32),
            sds((352, HALF), BF),
        ]
        + [sds((160, HALF), BF)] * 3,
        compiler_params=params(28),
        cost_estimate=cost(2 * TOK * D * 3 * LW, (3 * LW * D + 2 * TOK * D) * 2),
    )(dest, att_dq, d_kv, w3, *mixed, *mixed[2:])


def third_kernel(near_in, y0_in, left_in, right_in, x_in, y1_in, y2_in, y3_in, *refs):
    left_ref, right_ref, x_ref, y1_ref, y2_ref, y3_ref = refs
    y_in = (y1_in, y2_in, y3_in)
    outs = ((1, y1_ref), (2, y2_ref), (3, y3_ref))
    for t in range(2):
        rows, cols = slice(32 * t, 32 * t + 32), slice(COLS * t, COLS * (t + 1))
        mixed_left = left_in[rows, :]
        for ref in y_in:
            mixed_left = mixed_left + ref[128:, cols].astype(F32)
        mixed_left = mixed_left.astype(BF)
        last = (right_in[rows, 2 * COLS :] + x_in[320:, cols].astype(F32)).astype(BF)
        x_ref[64 + 32 * t : 96 + 32 * t, COLS:] = last
        for _, ref in outs:
            ref[64 + 32 * t : 96 + 32 * t, :COLS] = mixed_left
    x_ref[64:, :COLS] = (right_in[:, COLS : 2 * COLS] + x_in[256:320, COLS:].astype(F32)).astype(BF)
    middle = (right_in[:, :COLS] + x_in[256:320, :COLS].astype(F32)).astype(BF)
    for _, ref in outs:
        ref[64:, COLS:] = middle
    total = near_in[...].astype(F32) + x_in[:256].astype(F32)
    left_ref[...] = total[:64]
    for dy, ref in outs:
        ref[:64] = total[dy * 64 : (dy + 1) * 64].astype(BF)
    total = y0_in[...].astype(F32)
    for ref in y_in:
        total = total + ref[:128].astype(F32)
    right_ref[...] = total[:64]
    x_ref[:64] = total[64:].astype(BF)


def fourth_kernel(left_in, right_in, x_own, x_in, y_own, y1_in, y2_in, y3_in, x_ref, y_ref):
    y_in = (y1_in, y2_in, y3_in)
    left = left_in[...]
    for ref in y_in:
        left = left + ref[:64].astype(F32)
    y_ref[:64] = left.astype(BF)
    y_ref[64:128] = x_own[64:]
    y_ref[128:] = x_in[64:]
    x_ref[:64] = (right_in[...] + x_in[:64].astype(F32)).astype(BF)
    x_ref[64:128] = y_own[64:]
    for dy, ref in enumerate(y_in):
        x_ref[128 + dy * 64 : 192 + dy * 64] = ref[64:]


def fifth_kernel(x_own, x_in, y_own, y1_in, y2_in, y3_in, x_ref, y_ref):
    x_ref[:64] = y_own[:64]
    for dy, ref in enumerate((y1_in, y2_in, y3_in)):
        x_ref[64 + dy * 64 : 128 + dy * 64] = ref[:64]
    y_ref[:64] = x_own[:64]
    y_ref[64:] = x_in[:64]


def by_columns(kernel, tiles, mib, inputs, outputs):
    def tile(shape):
        return pl.BlockSpec((shape[0], shape[1] // tiles), lambda t: (0, t))

    return pl.pallas_call(
        kernel,
        grid=(tiles,),
        in_specs=[tile(a.shape) for a in inputs],
        out_specs=[tile((rows, HALF)) for rows, _ in outputs],
        out_shape=[sds((rows, HALF), dtype) for rows, dtype in outputs],
        compiler_params=params(mib),
        cost_estimate=cost(5e10, 4 << 20),
    )(*inputs)


def exchange(x, ys):
    return over_head(x, X_LO), [over_head(y, (dy, 0)) for dy, y in zip((1, 2, 3), ys)]


def place_kernel(first, src_ref, own_ref, beside_ref, y0_ref, y1_ref, y2_ref, y3_ref, out_ref):
    half = pl.program_id(0)

    def rows(i):
        return pl.ds(pl.multiple_of(src_ref[i] * 64, 64), 64)

    @pl.when(half == 0)
    def _():
        for dy, ref in enumerate((y0_ref, y1_ref, y2_ref, y3_ref)):
            out_ref[rows(dy), :] = ref[first : first + 64]
            out_ref[rows(4 + dy), :] = ref[first + 64 : first + 128]

    @pl.when(half == 1)
    def _():
        for dy in range(4):
            out_ref[rows(dy), :] = own_ref[first + dy * 64 : first + (dy + 1) * 64]
            out_ref[rows(4 + dy), :] = beside_ref[first + dy * 64 : first + (dy + 1) * 64]


def place(source, first, own, beside, ys):
    def whole(rows):
        return pl.BlockSpec((rows, HALF), lambda t, s: (0, 0))

    return pl.pallas_call(
        functools.partial(place_kernel, first),
        grid_spec=pltpu.PrefetchScalarGridSpec(
            num_scalar_prefetch=1,
            grid=(2,),
            in_specs=[whole(first + 256)] * 2 + [whole(first + 128)] * 4,
            out_specs=pl.BlockSpec((TOK, HALF), lambda t, s: (0, 1 - t)),
        ),
        out_shape=sds((TOK, D), BF),
        compiler_params=params(24),
        cost_estimate=cost(5e10, 4 * TOK * D),
    )(source, own, beside, *ys)


def turn_kernel(core_ref, x_ref, _, mine_ref, other_ref, scr):
    scr[...] = x_ref[...].T
    core = core_ref[0]
    for c in range(4):
        first = c * 2 * ROWS
        mine_ref[c] = scr[pl.ds(pl.multiple_of(first + core * ROWS, ROWS), ROWS), :]
        other_ref[c] = scr[pl.ds(pl.multiple_of(first + (1 - core) * ROWS, ROWS), ROWS), :]


def turn(core, x, before):
    block = pl.BlockSpec((4, ROWS, TOK), lambda c, s: (c, 0, 0))
    return pl.pallas_call(
        turn_kernel,
        grid_spec=pltpu.PrefetchScalarGridSpec(
            num_scalar_prefetch=1,
            grid=(2,),
            in_specs=[pl.BlockSpec((TOK, HALF), lambda c, s: (0, c)), pl.BlockSpec(memory_space=pl.ANY)],
            out_specs=[block, block],
            scratch_shapes=[pltpu.VMEM((HALF, TOK), BF)],
        ),
        out_shape=[sds((8, ROWS, TOK), BF)] * 2,
        compiler_params=params(),
        cost_estimate=cost(TOK * D * 64, 4 * TOK * D),
    )(core, x, before)


def weight_kernel(plan, n_lhs, n_rhs, *refs):
    lhs = refs[: 2 * n_lhs]
    rhs = refs[2 * n_lhs : 2 * n_lhs + n_rhs]
    out_ref = refs[-1]
    for pick, mine, theirs, dst in plan:
        left, right = (
            jnp.concatenate([ref[x_hi, z] for z in range(2) for x_hi in range(2)], axis=0)
            for ref in lhs[2 * pick : 2 * pick + 2]
        )
        out = dot(left, mine(rhs)) + dot(right, theirs(rhs))
        out_ref[:, dst : dst + out.shape[1]] = out.astype(BF)


def weight_terms(lhs_pairs, rhs, plan):
    lhs = [side.reshape(2, 4, ROWS, TOK) for pair in lhs_pairs for side in pair]
    rhs_specs = [pl.BlockSpec(r.shape, functools.partial(lambda nd, i: (0,) * nd, r.ndim)) for r in rhs]
    return pl.pallas_call(
        functools.partial(weight_kernel, plan, len(lhs_pairs), len(rhs)),
        grid=(2,),
        in_specs=[pl.BlockSpec((2, 2, ROWS, TOK), lambda i: (0, i, 0, 0))] * len(lhs) + rhs_specs,
        out_specs=pl.BlockSpec((4 * ROWS, 2 * LW), lambda i: (i, 0)),
        out_shape=sds((8 * ROWS, 2 * LW), BF),
        compiler_params=params(),
        cost_estimate=cost(2 * 8 * ROWS * 2 * TOK * 2 * LW, 10 << 20),
    )(*lhs, *rhs)


Z_GROUPS = [[x_hi * 8 + z * 2 + core for z in range(4)] for x_hi in range(2) for core in range(2)]
X_HI = view_route(lambda v: v + 8)


def weight_sum(x_hi, terms):
    total = lax.psum_scatter(terms, "view", scatter_dimension=0, axis_index_groups=Z_GROUPS, tiled=True)
    own = lax.dynamic_slice_in_dim(total, x_hi * ROWS, ROWS)
    other = lax.dynamic_slice_in_dim(total, (1 - x_hi) * ROWS, ROWS)
    return own, other


def with_x_hi(own, other):
    return own.astype(F32) + over_view(other, X_HI).astype(F32)


def local(x_tokens, w_qkv, w_out, grad_out):
    view = lax.axis_index("view")
    head = lax.axis_index("head")
    core = (view % 2).astype(jnp.int32)
    dest = jnp.stack([((head // 2 + dy) % 4) * 2 + (head % 2 ^ dx) for dy, dx in HEAD_STEPS]).astype(jnp.int32)
    source = jnp.stack([((head // 2 - dy) % 4) * 2 + (head % 2 ^ dx) for dy, dx in HEAD_STEPS]).astype(jnp.int32)
    core = core.reshape(1)
    w3 = jnp.transpose(w_qkv, (1, 0, 2))

    own = project_kv(x_tokens, w3)
    far = over_view(own, FAR)
    near = over_view(own, NEAR)
    beside = over_view(own, SWAP)

    queries = jnp.dot(x_tokens, w3[0], preferred_element_type=F32).astype(BF)
    d_att = jnp.dot(grad_out, w_out, preferred_element_type=F32).astype(BF)
    x_mine, x_other = turn(core, x_tokens, d_att)
    far, near, queries, d_att, x_mine, x_other = lax.optimization_barrier(
        (far, near, queries, d_att, x_mine, x_other)
    )
    relayed = over_view(far, SWAP)

    att_dq, d_own, d_near, d_swap, d_relay = attention(queries, d_att, (own, near, far, beside, relayed))

    back = over_view(d_swap, SWAP)
    mixed_near, mixed_far, mixed_y0, *mixed_y = mixed_product(dest, att_dq, w_out)
    mixed_x, mixed_y = exchange(mixed_far, mixed_y)

    relay = (d_relay + back[0].astype(F32)).astype(BF)
    two = over_view(d_near, FAR)
    one = over_view(relay, BACK_ONE)
    d_kv = (d_own + back[1].astype(F32) + two.astype(F32) + one.astype(F32)).astype(BF)

    near2, y02, left2, right2, x2, *y2 = input_product(
        dest, att_dq, d_kv, w3, (mixed_near, mixed_x, mixed_y0, *mixed_y)
    )
    from_x2, from_y2 = exchange(x2, y2)

    x_other, _ = lax.optimization_barrier((x_other, x2))
    x_theirs = over_view(x_other, SWAP)
    g_mine, g_other = turn(core, grad_out, x2)
    g_theirs = over_view(g_other, SWAP)
    att_dq_late, _ = lax.optimization_barrier((att_dq, x2))
    att_dq_theirs = over_view(att_dq_late, SWAP)
    early = weight_terms(
        [(x_mine, x_theirs), (g_mine, g_theirs)],
        [att_dq, att_dq_theirs],
        [(0, lambda r: r[0][1], lambda r: r[1][1], 0), (1, lambda r: r[0][0], lambda r: r[1][0], LW)],
    )
    early_own, early_other = weight_sum(view // 8, early)

    d_kv_late, _ = lax.optimization_barrier((d_kv, x2))
    d_kv_theirs = over_view(d_kv_late, SWAP)

    def columns(which, first):
        return lambda r: jnp.concatenate([r[which][h, :, first : first + E] for h in range(LH)], axis=1)

    late = weight_terms(
        [(x_mine, x_theirs)],
        [d_kv_late, d_kv_theirs],
        [(0, columns(0, 0), columns(1, 0), 0), (0, columns(0, E), columns(1, E), LW)],
    )
    late_sum = with_x_hi(*weight_sum(view // 8, late))

    near2, _, _ = lax.optimization_barrier((near2, late, g_mine))
    left3, right3, x3, *y3 = by_columns(
        third_kernel,
        1,
        56,
        (near2, y02, left2, right2, from_x2, *from_y2),
        [(64, F32), (64, F32), (128, BF), (128, BF), (128, BF), (128, BF)],
    )
    from_x3, from_y3 = exchange(x3, y3)
    left3, _ = lax.optimization_barrier((left3, early))
    x4, y4 = by_columns(
        fourth_kernel, 2, 16, (left3, right3, x3, from_x3, y3[0], *from_y3), [(320, BF), (192, BF)]
    )
    from_x4, from_y4 = exchange(x4, [y4] * 3)
    x4, late_sum = lax.optimization_barrier((x4, late_sum))
    x5, y5 = by_columns(fifth_kernel, 2, 16, (x4, from_x4, y4, *from_y4), [(256, BF), (128, BF)])
    early_other, _ = lax.optimization_barrier((early_other, x5))
    early_sum = with_x_hi(early_own, early_other)
    from_x5, from_y5 = exchange(x5, [y5] * 3)
    mixed_out = place(source, 64, x4, from_x4, (y4, *from_y4))
    d_input = place(source, 0, x5, from_x5, (y5, *from_y5))

    d_w = jnp.stack([early_sum[:, :LW], late_sum[:, :LW], late_sum[:, LW:]], axis=1)
    return (mixed_out, d_input, d_w, early_sum[:, LW:])


def solution(mesh):
    placed = (P("view", None), P(None, None, "head"), P(None, "head"), P("view", None))
    return jax.shard_map(
        local,
        mesh=mesh,
        in_specs=placed,
        out_specs=(P("view", None), P("view", None), P("view", None, "head"), P("view", "head")),
        check_vma=False,
    )
```

```python
import functools
import math

import jax
import jax.numpy as jnp
from jax import lax
from jax.experimental import pallas as pl
from jax.experimental.pallas import tpu as pltpu
from jax.sharding import PartitionSpec as P

D = 3072
HEADS = 24
E = 128
TOK = 512
LH = 3
LW = LH * E
ROWS = D // 16
SCALE = 1.0 / math.sqrt(E)
EXP2_SCALE = SCALE * math.log2(math.e)
BF = jnp.bfloat16
F32 = jnp.float32


def sds(shape, dtype):
    return jax.ShapeDtypeStruct(shape, dtype)


def dot(a, b, dims=((1,), (0,))):
    return lax.dot_general(a, b, (dims, ((), ())), preferred_element_type=F32)


def params(mib=56):
    return pltpu.CompilerParams(vmem_limit_bytes=mib << 20)


def cost(flops, moved, exps=0):
    return pl.CostEstimate(flops=int(flops), bytes_accessed=int(moved), transcendentals=int(exps))


def view_route(step):
    return [(v, step(v) % 16) for v in range(16)]


SWAP = view_route(lambda v: v ^ 1)
NEAR = view_route(lambda v: v + 2 if v % 2 == 0 else v - 2)
FAR = view_route(lambda v: v - 2 if v % 2 == 0 else v + 2)


BACK_ONE = view_route(lambda v: v - 1 if v % 2 == 0 else v + 1)
HEAD_STEPS = [(dy, dx) for dx in range(2) for dy in range(4)]
HALF = D // 2
X_LO = (0, 1)


def head_route(dy, dx):
    return [(h, ((h // 2 + dy) % 4) * 2 + (h % 2 ^ dx)) for h in range(8)]


def over_view(block, route):
    return lax.ppermute(block, "view", route)


def over_head(block, step):
    return lax.ppermute(block, "head", head_route(*step))


def kv_kernel(x_ref, wk_ref, wv_ref, kv_ref, acc):
    step = pl.program_id(0)
    x = x_ref[...]
    k = dot(x, wk_ref[...])
    v = dot(x, wv_ref[...])

    @pl.when(step == 0)
    def _():
        acc[:, :LW] = k
        acc[:, LW:] = v

    @pl.when(step == 1)
    def _():
        for h in range(LH):
            cols = slice(h * E, (h + 1) * E)
            kv_ref[h, :, :E] = (acc[:, cols] + k[:, cols]).astype(BF)
            kv_ref[h, :, E:] = (acc[:, LW + h * E : LW + (h + 1) * E] + v[:, cols]).astype(BF)


def project_kv(x, w3):
    depth = D // 2
    return pl.pallas_call(
        kv_kernel,
        grid=(2,),
        in_specs=[
            pl.BlockSpec((TOK, depth), lambda i: (0, i)),
            pl.BlockSpec((None, depth, LW), lambda i: (1, i, 0)),
            pl.BlockSpec((None, depth, LW), lambda i: (2, i, 0)),
        ],
        out_specs=pl.BlockSpec((LH, TOK, 2 * E), lambda i: (0, 0, 0)),
        out_shape=sds((LH, TOK, 2 * E), BF),
        scratch_shapes=[pltpu.VMEM((TOK, 2 * LW), F32)],
        compiler_params=params(),
        cost_estimate=cost(2 * TOK * D * 2 * LW, 9 << 20),
    )(x, w3, w3)


def attention_kernel(q_ref, g_ref, o_ref, a_ref, b_ref, c_ref, r_ref, *refs):
    att_dq_ref, d_o, d_a, d_bc, d_r, s_scr, dp_scr = refs[-7:]
    n = TOK
    kvs = (o_ref, a_ref, b_ref, c_ref, r_ref)
    outs = (d_o, d_a, d_bc.at[0], d_bc.at[1], d_r)
    q = q_ref[...]
    g = g_ref[...]
    q_t = q.T
    g_t = g.T
    top = None
    for j, kv in enumerate(kvs):
        s = dot(kv[:, :E], q_t)
        s_scr[j * n : (j + 1) * n] = s
        here = jnp.max(s, axis=0, keepdims=True)
        top = here if top is None else jnp.maximum(top, here)
    top = top * EXP2_SCALE
    total = None
    for j in range(5):
        e = jnp.exp2(s_scr[j * n : (j + 1) * n] * EXP2_SCALE - top)
        s_scr[j * n : (j + 1) * n] = e
        here = jnp.sum(e, axis=0, keepdims=True)
        total = here if total is None else total + here
    inverse = 1.0 / total
    delta = None
    acc = None
    for j, kv in enumerate(kvs):
        p = s_scr[j * n : (j + 1) * n] * inverse
        s_scr[j * n : (j + 1) * n] = p
        p_bf = p.astype(BF)
        v = kv[:, E:]
        dp = dot(v, g_t)
        dp_scr[j * n : (j + 1) * n] = dp
        here = jnp.sum(p * dp, axis=0, keepdims=True)
        delta = here if delta is None else delta + here
        term = dot(v.T, p_bf)
        acc = term if acc is None else acc + term
        outs[j][:, E:] = dot(p_bf, g).astype(outs[j].dtype)
    att_dq_ref[0] = acc.T.astype(BF)
    acc = None
    for j, kv in enumerate(kvs):
        ds = (s_scr[j * n : (j + 1) * n] * (dp_scr[j * n : (j + 1) * n] - delta) * SCALE).astype(BF)
        k = kv[:, :E]
        term = dot(k.T, ds)
        acc = term if acc is None else acc + term
        outs[j][:, :E] = dot(ds, q).astype(outs[j].dtype)
    att_dq_ref[1] = acc.T.astype(BF)


def attention(queries, d_att, kvs):
    head_block = pl.BlockSpec((TOK, E), lambda h: (0, h))
    pair = pl.BlockSpec((None, TOK, 2 * E), lambda h: (h, 0, 0))
    return pl.pallas_call(
        attention_kernel,
        grid=(LH,),
        in_specs=[head_block, head_block] + [pair] * 5,
        out_specs=[
            pl.BlockSpec((2, TOK, E), lambda h: (0, 0, h)),
            pair,
            pair,
            pl.BlockSpec((2, None, TOK, 2 * E), lambda h: (0, h, 0, 0)),
            pair,
        ],
        out_shape=[
            sds((2, TOK, LW), BF),
            sds((LH, TOK, 2 * E), F32),
            sds((LH, TOK, 2 * E), BF),
            sds((2, LH, TOK, 2 * E), BF),
            sds((LH, TOK, 2 * E), F32),
        ],
        scratch_shapes=[pltpu.VMEM((5 * TOK, TOK), F32)] * 2,
        compiler_params=params(),
        cost_estimate=cost(LH * 6 * 2 * TOK * 5 * TOK * E * 2, 12 << 20, LH * 5 * TOK * TOK),
    )(queries, d_att, *kvs)


COLS = D // 4


def left_tile(rows):
    return pl.BlockSpec((rows, COLS), lambda t, *s: (0, jnp.minimum(t, 1)))


def right_tile(rows):
    return pl.BlockSpec((rows, COLS), lambda t, *s: (0, jnp.maximum(t - 2, 0)))


def gather_rows(dest_ref, a_scr, pieces):
    for i in range(8):
        rows = pl.ds(pl.multiple_of(dest_ref[i] * 64, 64), 64)
        for at, part in pieces:
            a_scr[i * 64 : (i + 1) * 64, at : at + part.shape[1]] = part[rows, :]


def y_rows(out, dy):
    return out[dy * 64 : (dy + 1) * 64], out[256 + dy * 64 : 256 + (dy + 1) * 64]


def mixed_kernel(dest_ref, att_ref, w_ref, near_ref, far_ref, y0_ref, y1_ref, y2_ref, y3_ref, a_scr):
    tile = pl.program_id(0)

    @pl.when(tile == 0)
    def _():
        gather_rows(dest_ref, a_scr, [(0, att_ref)])

    out = dot(a_scr[...], w_ref[...], ((1,), (1,))).astype(BF)

    @pl.when(tile == 0)
    def _():
        near_ref[...] = out[:256]
        far_ref[...] = out[256:]

    @pl.when(tile > 0)
    def _():
        for dy, ref in enumerate((y0_ref, y1_ref, y2_ref, y3_ref)):
            ref[:64], ref[64:] = y_rows(out, dy)


def mixed_product(dest, att_dq, w_out):
    return pl.pallas_call(
        mixed_kernel,
        grid_spec=pltpu.PrefetchScalarGridSpec(
            num_scalar_prefetch=1,
            grid=(4,),
            in_specs=[
                pl.BlockSpec((None, TOK, LW), lambda t, s: (0, 0, 0)),
                pl.BlockSpec((COLS, LW), lambda t, s: (t, 0)),
            ],
            out_specs=[pl.BlockSpec((256, COLS), lambda t, s: (0, 0))] * 2
            + [pl.BlockSpec((128, COLS), lambda t, s: (0, jnp.maximum(t - 1, 0)))] * 4,
            scratch_shapes=[pltpu.VMEM((TOK, LW), BF)],
        ),
        out_shape=[sds((256, COLS), BF)] * 2 + [sds((128, 3 * COLS), BF)] * 4,
        compiler_params=params(24),
        cost_estimate=cost(2 * TOK * D * LW, (LW * D + TOK * D) * 2),
    )(dest, att_dq, w_out)


def input_kernel(dest_ref, *refs):
    dq_ref, d_kv_ref, w_ref, near_in, far_in = refs[:5]
    y_in, y_last = refs[5:9], refs[9:13]
    near_ref, y0_ref, left_ref, right_ref, x_ref, y1_ref, y2_ref, y3_ref, a_scr = refs[13:]
    tile = pl.program_id(0)

    @pl.when(tile == 0)
    def _():
        pieces = [(0, dq_ref)]
        for h in range(LH):
            pieces += [(LW + E * h, d_kv_ref.at[h, :, :E]), (2 * LW + E * h, d_kv_ref.at[h, :, E:])]
        gather_rows(dest_ref, a_scr, pieces)

    a = a_scr[...]
    out = None
    for i in range(3):
        term = dot(a[:, i * LW : (i + 1) * LW], w_ref[i], ((1,), (1,)))
        out = term if out is None else out + term
    out = out.astype(BF)

    def total_of(parts, rows):
        total = parts[0][rows, :].astype(F32)
        for ref in parts[1:]:
            total = total + ref[rows, :].astype(F32)
        return total

    @pl.when(tile < 2)
    def _():
        near_ref[...] = out[:256]
        x_ref[:256] = out[256:]
        total = total_of(y_in, slice(0, 128))
        right_ref[...] = total[:64]
        x_ref[256:320] = total[64:].astype(BF)

    for t in range(2):
        @pl.when(tile == t)
        def _():
            x_ref[320:] = total_of(y_last, slice(64 + 32 * t, 96 + 32 * t)).astype(BF)

    @pl.when(tile == 2)
    def _():
        right_ref[...] = total_of(y_last, slice(0, 64))

    for t in range(2):
        @pl.when(tile == 2 + t)
        def _():
            total = near_in[...].astype(F32) + far_in[...].astype(F32)
            left_ref[...] = total[:64]
            y0_ref[:64], y0_ref[64:] = y_rows(out, 0)
            for dy, ref in ((1, y1_ref), (2, y2_ref), (3, y3_ref)):
                ref[:64], ref[64:128] = y_rows(out, dy)
                ref[128:] = total[dy * 64 + 32 * t : dy * 64 + 32 * t + 32].astype(BF)


def input_product(dest, att_dq, d_kv, w3, mixed):
    return pl.pallas_call(
        input_kernel,
        grid_spec=pltpu.PrefetchScalarGridSpec(
            num_scalar_prefetch=1,
            grid=(4,),
            in_specs=[
                pl.BlockSpec((None, TOK, LW), lambda t, s: (1, 0, 0)),
                pl.BlockSpec((LH, TOK, 2 * E), lambda t, s: (0, 0, 0)),
                pl.BlockSpec((3, COLS, LW), lambda t, s: (0, t, 0)),
            ]
            + [pl.BlockSpec((256, COLS), lambda t, s: (0, 0))] * 2
            + [left_tile(128)] * 4
            + [pl.BlockSpec((128, COLS), lambda t, s: (0, 2))] * 4,
            out_specs=[
                left_tile(256),
                right_tile(128),
                pl.BlockSpec((64, COLS), lambda t, s: (0, 0)),
                pl.BlockSpec((64, COLS), lambda t, s: (0, jnp.minimum(t, 2))),
                left_tile(352),
            ]
            + [right_tile(160)] * 3,
            scratch_shapes=[pltpu.VMEM((TOK, 3 * LW), BF)],
        ),
        out_shape=[
            sds((256, HALF), BF),
            sds((128, HALF), BF),
            sds((64, COLS), F32),
            sds((64, 3 * COLS), F32),
            sds((352, HALF), BF),
        ]
        + [sds((160, HALF), BF)] * 3,
        compiler_params=params(28),
        cost_estimate=cost(2 * TOK * D * 3 * LW, (3 * LW * D + 2 * TOK * D) * 2),
    )(dest, att_dq, d_kv, w3, *mixed, *mixed[2:])


def third_kernel(near_in, y0_in, left_in, right_in, x_in, y1_in, y2_in, y3_in, *refs):
    left_ref, right_ref, x_ref, y1_ref, y2_ref, y3_ref = refs
    y_in = (y1_in, y2_in, y3_in)
    outs = ((1, y1_ref), (2, y2_ref), (3, y3_ref))
    for t in range(2):
        rows, cols = slice(32 * t, 32 * t + 32), slice(COLS * t, COLS * (t + 1))
        mixed_left = left_in[rows, :]
        for ref in y_in:
            mixed_left = mixed_left + ref[128:, cols].astype(F32)
        mixed_left = mixed_left.astype(BF)
        last = (right_in[rows, 2 * COLS :] + x_in[320:, cols].astype(F32)).astype(BF)
        x_ref[64 + 32 * t : 96 + 32 * t, COLS:] = last
        for _, ref in outs:
            ref[64 + 32 * t : 96 + 32 * t, :COLS] = mixed_left
    x_ref[64:, :COLS] = (right_in[:, COLS : 2 * COLS] + x_in[256:320, COLS:].astype(F32)).astype(BF)
    middle = (right_in[:, :COLS] + x_in[256:320, :COLS].astype(F32)).astype(BF)
    for _, ref in outs:
        ref[64:, COLS:] = middle
    total = near_in[...].astype(F32) + x_in[:256].astype(F32)
    left_ref[...] = total[:64]
    for dy, ref in outs:
        ref[:64] = total[dy * 64 : (dy + 1) * 64].astype(BF)
    total = y0_in[...].astype(F32)
    for ref in y_in:
        total = total + ref[:128].astype(F32)
    right_ref[...] = total[:64]
    x_ref[:64] = total[64:].astype(BF)


def fourth_kernel(left_in, right_in, x_own, x_in, y_own, y1_in, y2_in, y3_in, x_ref, y_ref):
    y_in = (y1_in, y2_in, y3_in)
    left = left_in[...]
    for ref in y_in:
        left = left + ref[:64].astype(F32)
    y_ref[:64] = left.astype(BF)
    y_ref[64:128] = x_own[64:]
    y_ref[128:] = x_in[64:]
    x_ref[:64] = (right_in[...] + x_in[:64].astype(F32)).astype(BF)
    x_ref[64:128] = y_own[64:]
    for dy, ref in enumerate(y_in):
        x_ref[128 + dy * 64 : 192 + dy * 64] = ref[64:]


def fifth_kernel(x_own, x_in, y_own, y1_in, y2_in, y3_in, x_ref, y_ref):
    x_ref[:64] = y_own[:64]
    for dy, ref in enumerate((y1_in, y2_in, y3_in)):
        x_ref[64 + dy * 64 : 128 + dy * 64] = ref[:64]
    y_ref[:64] = x_own[:64]
    y_ref[64:] = x_in[:64]


def by_columns(kernel, tiles, mib, inputs, outputs):
    def tile(shape):
        return pl.BlockSpec((shape[0], shape[1] // tiles), lambda t: (0, t))

    return pl.pallas_call(
        kernel,
        grid=(tiles,),
        in_specs=[tile(a.shape) for a in inputs],
        out_specs=[tile((rows, HALF)) for rows, _ in outputs],
        out_shape=[sds((rows, HALF), dtype) for rows, dtype in outputs],
        compiler_params=params(mib),
        cost_estimate=cost(5e10, 4 << 20),
    )(*inputs)


def exchange(x, ys):
    return over_head(x, X_LO), [over_head(y, (dy, 0)) for dy, y in zip((1, 2, 3), ys)]


def place_kernel(first, src_ref, own_ref, beside_ref, y0_ref, y1_ref, y2_ref, y3_ref, out_ref):
    half = pl.program_id(0)

    def rows(i):
        return pl.ds(pl.multiple_of(src_ref[i] * 64, 64), 64)

    @pl.when(half == 0)
    def _():
        for dy, ref in enumerate((y0_ref, y1_ref, y2_ref, y3_ref)):
            out_ref[rows(dy), :] = ref[first : first + 64]
            out_ref[rows(4 + dy), :] = ref[first + 64 : first + 128]

    @pl.when(half == 1)
    def _():
        for dy in range(4):
            out_ref[rows(dy), :] = own_ref[first + dy * 64 : first + (dy + 1) * 64]
            out_ref[rows(4 + dy), :] = beside_ref[first + dy * 64 : first + (dy + 1) * 64]


def place(source, first, own, beside, ys):
    def whole(rows):
        return pl.BlockSpec((rows, HALF), lambda t, s: (0, 0))

    return pl.pallas_call(
        functools.partial(place_kernel, first),
        grid_spec=pltpu.PrefetchScalarGridSpec(
            num_scalar_prefetch=1,
            grid=(2,),
            in_specs=[whole(first + 256)] * 2 + [whole(first + 128)] * 4,
            out_specs=pl.BlockSpec((TOK, HALF), lambda t, s: (0, 1 - t)),
        ),
        out_shape=sds((TOK, D), BF),
        compiler_params=params(24),
        cost_estimate=cost(5e10, 4 * TOK * D),
    )(source, own, beside, *ys)


def turn_kernel(core_ref, x_ref, _, mine_ref, other_ref, scr):
    scr[...] = x_ref[...].T
    core = core_ref[0]
    for c in range(4):
        first = c * 2 * ROWS
        mine_ref[c] = scr[pl.ds(pl.multiple_of(first + core * ROWS, ROWS), ROWS), :]
        other_ref[c] = scr[pl.ds(pl.multiple_of(first + (1 - core) * ROWS, ROWS), ROWS), :]


def turn(core, x, before):
    block = pl.BlockSpec((4, ROWS, TOK), lambda c, s: (c, 0, 0))
    return pl.pallas_call(
        turn_kernel,
        grid_spec=pltpu.PrefetchScalarGridSpec(
            num_scalar_prefetch=1,
            grid=(2,),
            in_specs=[pl.BlockSpec((TOK, HALF), lambda c, s: (0, c)), pl.BlockSpec(memory_space=pl.ANY)],
            out_specs=[block, block],
            scratch_shapes=[pltpu.VMEM((HALF, TOK), BF)],
        ),
        out_shape=[sds((8, ROWS, TOK), BF)] * 2,
        compiler_params=params(),
        cost_estimate=cost(TOK * D * 64, 4 * TOK * D),
    )(core, x, before)


def weight_kernel(plan, n_lhs, n_rhs, *refs):
    lhs = refs[: 2 * n_lhs]
    rhs = refs[2 * n_lhs : 2 * n_lhs + n_rhs]
    out_ref = refs[-1]
    for pick, mine, theirs, dst in plan:
        left, right = (
            jnp.concatenate([ref[x_hi, z] for z in range(2) for x_hi in range(2)], axis=0)
            for ref in lhs[2 * pick : 2 * pick + 2]
        )
        out = dot(left, mine(rhs)) + dot(right, theirs(rhs))
        out_ref[:, dst : dst + out.shape[1]] = out.astype(BF)


def weight_terms(lhs_pairs, rhs, plan):
    lhs = [side.reshape(2, 4, ROWS, TOK) for pair in lhs_pairs for side in pair]
    rhs_specs = [pl.BlockSpec(r.shape, functools.partial(lambda nd, i: (0,) * nd, r.ndim)) for r in rhs]
    return pl.pallas_call(
        functools.partial(weight_kernel, plan, len(lhs_pairs), len(rhs)),
        grid=(2,),
        in_specs=[pl.BlockSpec((2, 2, ROWS, TOK), lambda i: (0, i, 0, 0))] * len(lhs) + rhs_specs,
        out_specs=pl.BlockSpec((4 * ROWS, 2 * LW), lambda i: (i, 0)),
        out_shape=sds((8 * ROWS, 2 * LW), BF),
        compiler_params=params(),
        cost_estimate=cost(2 * 8 * ROWS * 2 * TOK * 2 * LW, 10 << 20),
    )(*lhs, *rhs)


Z_GROUPS = [[x_hi * 8 + z * 2 + core for z in range(4)] for x_hi in range(2) for core in range(2)]
X_HI = view_route(lambda v: v + 8)


def weight_sum(x_hi, terms):
    total = lax.psum_scatter(terms, "view", scatter_dimension=0, axis_index_groups=Z_GROUPS, tiled=True)
    own = lax.dynamic_slice_in_dim(total, x_hi * ROWS, ROWS)
    other = lax.dynamic_slice_in_dim(total, (1 - x_hi) * ROWS, ROWS)
    return own, other


def with_x_hi(own, other):
    return own.astype(F32) + over_view(other, X_HI).astype(F32)


def local(x_tokens, w_qkv, w_out, grad_out):
    view = lax.axis_index("view")
    head = lax.axis_index("head")
    core = (view % 2).astype(jnp.int32)
    dest = jnp.stack([((head // 2 + dy) % 4) * 2 + (head % 2 ^ dx) for dy, dx in HEAD_STEPS]).astype(jnp.int32)
    source = jnp.stack([((head // 2 - dy) % 4) * 2 + (head % 2 ^ dx) for dy, dx in HEAD_STEPS]).astype(jnp.int32)
    core = core.reshape(1)
    w3 = jnp.transpose(w_qkv, (1, 0, 2))

    own = project_kv(x_tokens, w3)
    far = over_view(own, FAR)
    near = over_view(own, NEAR)
    beside = over_view(own, SWAP)

    queries = jnp.dot(x_tokens, w3[0], preferred_element_type=F32).astype(BF)
    d_att = jnp.dot(grad_out, w_out, preferred_element_type=F32).astype(BF)
    x_mine, x_other = turn(core, x_tokens, d_att)
    far, near, queries, d_att, x_mine, x_other = lax.optimization_barrier(
        (far, near, queries, d_att, x_mine, x_other)
    )
    relayed = over_view(far, SWAP)

    att_dq, d_own, d_near, d_swap, d_relay = attention(queries, d_att, (own, near, far, beside, relayed))

    back = over_view(d_swap, SWAP)
    mixed_near, mixed_far, mixed_y0, *mixed_y = mixed_product(dest, att_dq, w_out)
    mixed_x, mixed_y = exchange(mixed_far, mixed_y)

    d_relay, _ = lax.optimization_barrier((d_relay, mixed_far))
    relay = (d_relay + back[0].astype(F32)).astype(BF)
    two = over_view(d_near, FAR)
    one = over_view(relay, BACK_ONE)
    d_kv = (d_own + back[1].astype(F32) + two.astype(F32) + one.astype(F32)).astype(BF)

    near2, y02, left2, right2, x2, *y2 = input_product(
        dest, att_dq, d_kv, w3, (mixed_near, mixed_x, mixed_y0, *mixed_y)
    )
    from_x2, from_y2 = exchange(x2, y2)

    x_other, _ = lax.optimization_barrier((x_other, x2))
    x_theirs = over_view(x_other, SWAP)
    g_mine, g_other = turn(core, grad_out, x2)
    g_theirs = over_view(g_other, SWAP)
    att_dq_late, _ = lax.optimization_barrier((att_dq, x2))
    att_dq_theirs = over_view(att_dq_late, SWAP)
    early = weight_terms(
        [(x_mine, x_theirs), (g_mine, g_theirs)],
        [att_dq, att_dq_theirs],
        [(0, lambda r: r[0][1], lambda r: r[1][1], 0), (1, lambda r: r[0][0], lambda r: r[1][0], LW)],
    )
    early_own, early_other = weight_sum(view // 8, early)

    d_kv_late, _ = lax.optimization_barrier((d_kv, x2))
    d_kv_theirs = over_view(d_kv_late, SWAP)

    def columns(which, first):
        return lambda r: jnp.concatenate([r[which][h, :, first : first + E] for h in range(LH)], axis=1)

    late = weight_terms(
        [(x_mine, x_theirs)],
        [d_kv_late, d_kv_theirs],
        [(0, columns(0, 0), columns(1, 0), 0), (0, columns(0, E), columns(1, E), LW)],
    )
    late_sum = with_x_hi(*weight_sum(view // 8, late))

    near2, _, _ = lax.optimization_barrier((near2, late, g_mine))
    left3, right3, x3, *y3 = by_columns(
        third_kernel,
        1,
        56,
        (near2, y02, left2, right2, from_x2, *from_y2),
        [(64, F32), (64, F32), (128, BF), (128, BF), (128, BF), (128, BF)],
    )
    from_x3, from_y3 = exchange(x3, y3)
    left3, _ = lax.optimization_barrier((left3, early))
    x4, y4 = by_columns(
        fourth_kernel, 2, 16, (left3, right3, x3, from_x3, y3[0], *from_y3), [(320, BF), (192, BF)]
    )
    from_x4, from_y4 = exchange(x4, [y4] * 3)
    x4, late_sum = lax.optimization_barrier((x4, late_sum))
    x5, y5 = by_columns(fifth_kernel, 2, 16, (x4, from_x4, y4, *from_y4), [(256, BF), (128, BF)])
    early_other, _ = lax.optimization_barrier((early_other, x5))
    early_sum = with_x_hi(early_own, early_other)
    from_x5, from_y5 = exchange(x5, [y5] * 3)
    mixed_out = place(source, 64, x4, from_x4, (y4, *from_y4))
    d_input = place(source, 0, x5, from_x5, (y5, *from_y5))

    d_w = jnp.stack([early_sum[:, :LW], late_sum[:, :LW], late_sum[:, LW:]], axis=1)
    return (mixed_out, d_input, d_w, early_sum[:, LW:])


def solution(mesh):
    placed = (P("view", None), P(None, None, "head"), P(None, "head"), P("view", None))
    return jax.shard_map(
        local,
        mesh=mesh,
        in_specs=placed,
        out_specs=(P("view", None), P("view", None), P("view", None, "head"), P("view", "head")),
        check_vma=False,
    )
```
